32 devices in a mesh: ctx: 8 (over y, x, core), head: 4 (over z).
Axes of the slice: x: 2, y: 2, z: 4, core: 2. Of those that a mesh axis runs over, the one named last changes fastest.
Arguments:
- q_prompt: bfloat16 [4096, 32, 256], P('ctx', 'head'), may hold values from -0.3984375 to 0.3984375
- k_prompt: bfloat16 [4096, 32, 256], P('ctx', 'head'), may hold values from -0.3984375 to 0.3984375
- v_prompt: bfloat16 [4096, 32, 256], P('ctx', 'head'), may hold values from -6 to 6
- log_decay: float32 [32, 4096], P('head', 'ctx'), may hold values from -1 to 0
- prompt_section: int32 [256, 1], P('ctx'), may hold values from 0 to 7; in each aligned block of 32 rows (0 to 31, 32 to 63, ...) at most 4 rows name the same one
- q_step: bfloat16 [256, 4, 32, 256], P('ctx', None, 'head'), may hold values from -0.3984375 to 0.3984375
- k_step: bfloat16 [256, 4, 32, 256], P('ctx', None, 'head'), may hold values from -3 to 3
- v_step: bfloat16 [256, 4, 32, 256], P('ctx', None, 'head'), may hold values from -6 to 6
- step_decay: float32 [32, 4, 256], P('head', None, 'ctx'), may hold values from -0.6 to -0.05
- w_out: bfloat16 [8192, 8192], P(None, 'head'), may hold values from -0.0625 to 0.0625
Outputs:
- prompt_out: bfloat16 [4096, 8192], P('ctx', 'head')
- step_out: bfloat16 [256, 4, 8192], P('ctx', None, 'head')
The draws below stay inside these ranges and needn't reach their ends.
Inputs may be any that keep to these rules, and one draw needn't show every extreme that they name: `prompt_section`: among the rows of one index of ctx, no section is named more than 4 times.
All inputs are finite; a program needn't handle non-finite values.
Results may differ from the reference program's by a relative error of at most 0.015.
Values may be sent and summed in bfloat16 or wider, within the bound.
A program may use at most 128 MiB of HBM per device.

```python
import math
import jax
import jax.numpy as jnp
import numpy as np
from jax import lax

D = 8192
RETENTION_HEADS = 32
HD = 256
BLOCK = 512
STEPS = 4
TOK_DEV = 512
ROWS_DEV = 32
CAP = 4
PROMPT_TOKENS = 4096
ROWS = 256
N_CTX = 8


def draw_log_decay(key, part):
    random_subkey_list = jax.random.split(key, 7)
    fast_share = 0.5
    head_draw = jax.random.uniform(random_subkey_list[0], (RETENTION_HEADS, 1), jnp.float32)
    is_fast = head_draw < fast_share
    fast_rate = jnp.exp(jax.random.uniform(random_subkey_list[1], (RETENTION_HEADS, 1), jnp.float32, jnp.log(1.0 / 50.0), jnp.log(1.0 / 30.0)))
    slow_rate = jnp.exp(jax.random.uniform(random_subkey_list[2], (RETENTION_HEADS, 1), jnp.float32, jnp.log(0.1), jnp.log(0.5))) / PROMPT_TOKENS
    baseline_decay_rate = jnp.where(is_fast, fast_rate, slow_rate)
    rough_decay = jnp.exp(jax.random.uniform(random_subkey_list[3], (RETENTION_HEADS, 64), jnp.float32, jnp.log(0.5), jnp.log(2.0)))
    rough_decay = jnp.repeat(rough_decay, PROMPT_TOKENS // 64, axis=1)
    random_wobble = jax.random.uniform(random_subkey_list[4], (RETENTION_HEADS, PROMPT_TOKENS), jnp.float32, 0.5, 1.5)
    decay_spikes = jax.random.uniform(random_subkey_list[5], (RETENTION_HEADS, PROMPT_TOKENS), jnp.float32) < 3.0 / PROMPT_TOKENS
    spike_log_decay = jnp.log(jax.random.uniform(random_subkey_list[6], (RETENTION_HEADS, PROMPT_TOKENS), jnp.float32, 0.5, 0.8))
    return (-baseline_decay_rate * rough_decay * random_wobble + jnp.where(decay_spikes, spike_log_decay, 0.0)).astype(jnp.float32)


def block_levels(rng, dims, pieces, least, high):
    factor_of, own = 1.0, jax.random.fold_in(rng, 6)
    for position, parts in pieces:
        steps = jnp.exp(jax.random.uniform(jax.random.fold_in(own, position), (parts,), jnp.float32, least / len(pieces), high / len(pieces)))
        factor_of = factor_of * jnp.repeat(steps, dims[position] // parts).reshape([-1 if axis == position else 1 for axis in range(len(dims))])
    return factor_of


def assign_block(key, own, number, rows, count, top, most, lean):
    ranking = jax.random.permutation(key, count)
    packed, ordinary = portions_of(count, rows * top, most, lean, True), portions_of(count, rows * top, most, lean, False)
    places = jnp.arange(count)

    def named(lengths, turn):
        used = int((lengths > 0).sum())
        fixed = max(1, used // 4)
        shifted = fixed + (places - fixed + turn * (used - fixed)) % max(1, count - fixed)
        return jnp.zeros((count,), jnp.int32).at[ranking[jnp.where(places < fixed, places, shifted)]].set(jnp.asarray(lengths, jnp.int32))

    lengths = jnp.where(number % 4 == 0, named(packed, number // 4), named(ordinary, number - number // 4 - 1))
    mixed = jax.random.permutation(jax.random.fold_in(own, 3), count)
    giver, taker = mixed[0:count // 2 * 2:2], mixed[1:count // 2 * 2:2]
    slack = jnp.minimum(lengths[giver] - 1, most - lengths[taker]) // 2
    slack = jnp.where((giver == ranking[0]) | (taker == ranking[0]) | (lengths[taker] == 0), 0, jnp.maximum(slack, 0))
    shifted = jax.random.randint(jax.random.fold_in(own, 4), (count // 2,), 0, 1 << 20) % (slack + 1)
    lengths = lengths.at[giver].add(-shifted).at[taker].add(shifted)
    members = jnp.searchsorted(jnp.cumsum(lengths), jnp.arange(rows * top), side="right").astype(jnp.int32)
    table = members.reshape(top, rows).T
    table = table[jax.random.permutation(jax.random.fold_in(own, 1), rows)]
    turn = jax.random.randint(jax.random.fold_in(own, 2), (rows, 1), 0, top)
    return jnp.take_along_axis(table, (jnp.arange(top)[None, :] + turn) % top, axis=1)


def portions_of(count, total, reach, skew, full):
    loads = [(1 << 20) // math.isqrt(rank ** skew) + 1 for rank in range(1, count + 1)]
    largest = reach if full else min(reach, max(-(-total // count), total * loads[0] // sum(loads)))
    least = 1 if total - largest >= count - 1 else 0
    holding, surplus = [largest] + [least] * (count - 1), total - largest - least * (count - 1)
    while surplus > 0:
        free = [i for i in range(1, count) if holding[i] < largest] or [i for i in range(1, count) if holding[i] < reach]
        mass, remaining = sum([loads[i] for i in free]), surplus
        for i in free:
            more = min(reach - holding[i], max(1, remaining * loads[i] // mass), surplus)
            holding[i] = holding[i] + more
            surplus = surplus - more
    return np.array(holding)


def bell_draw(rng, extent, deviation, limit, pieces=(), held_as=jnp.bfloat16):
    loudness = block_levels(rng, extent, pieces, -0.22, 0.18) if pieces else 1.0
    values = jax.random.normal(rng, extent, jnp.float32) * deviation * loudness
    return jnp.minimum(jnp.maximum(values, -limit), limit).astype(held_as)


def setup_inputs(seed: int = 0) -> dict:
    streams_of = jax.random.split(jax.random.key(seed), 11)
    q_prompt = bell_draw(streams_of[0], (PROMPT_TOKENS, RETENTION_HEADS, HD), 0.0625, 0.3984375, ((0, 8), (1, 4)))
    k_prompt = bell_draw(streams_of[1], (PROMPT_TOKENS, RETENTION_HEADS, HD), 0.0625, 0.3984375, ((0, 8), (1, 4)))
    v_prompt = bell_draw(streams_of[2], (PROMPT_TOKENS, RETENTION_HEADS, HD), 1.0, 6.0, ((0, 8), (1, 4)))
    log_decay = draw_log_decay(jax.random.fold_in(streams_of[10], 71), 0)
    prompt_section_keys = jax.random.split(jax.random.fold_in(streams_of[4], 1), ROWS // ROWS_DEV)
    prompt_section_turns = jax.random.permutation(jax.random.fold_in(streams_of[4], 3), ROWS // ROWS_DEV)
    prompt_section = jax.vmap(lambda own, number: assign_block(jax.random.fold_in(streams_of[4], 2), own, number, ROWS_DEV, N_CTX, 1, CAP, 1))(prompt_section_keys, prompt_section_turns).reshape((ROWS, 1))
    q_step = bell_draw(streams_of[5], (ROWS, STEPS, RETENTION_HEADS, HD), 0.0625, 0.3984375, ((0, 8), (2, 4)))
    k_step = bell_draw(streams_of[6], (ROWS, STEPS, RETENTION_HEADS, HD), 0.5, 3.0, ((0, 8), (2, 4)))
    v_step = bell_draw(streams_of[7], (ROWS, STEPS, RETENTION_HEADS, HD), 1.0, 6.0, ((0, 8), (2, 4)))
    step_decay = jnp.clip(-0.6 + 0.55 * jax.random.uniform(streams_of[8], (RETENTION_HEADS, STEPS, ROWS), jnp.float32) ** block_levels(streams_of[8], (RETENTION_HEADS, STEPS, ROWS), ((0, 4), (2, 8)), -0.2, 0.2), -0.6, -0.05)
    w_out = bell_draw(streams_of[9], (RETENTION_HEADS * HD, D), (RETENTION_HEADS * HD) ** -0.5, 0.0625, ((1, 4),))
    return {"q_prompt": q_prompt, "k_prompt": k_prompt, "v_prompt": v_prompt, "log_decay": log_decay, "prompt_section": prompt_section, "q_step": q_step, "k_step": k_step, "v_step": v_step, "step_decay": step_decay, "w_out": w_out}


def block_step(carry_state, block_pair):
    query_rows, key_matrix_rows, value_rows, log_rates = block_pair
    positions = jnp.arange(BLOCK)
    causal = positions[:, None] >= positions[None, :]
    cumlog = jnp.cumsum(log_rates, axis=1)
    decays = jnp.where(causal[None], jnp.exp(jnp.minimum(cumlog[:, :, None] - cumlog[:, None, :], 0.0)), 0.0)
    attention_scores = jnp.einsum('jsv,csv->sjc', query_rows.astype(jnp.float32), key_matrix_rows.astype(jnp.float32))
    weights = (attention_scores * decays).astype(jnp.bfloat16)
    within = jnp.einsum('hnm,mhe->nhe', weights.astype(jnp.float32), value_rows.astype(jnp.float32))
    carried = jnp.einsum('nhd,hde->nhe', query_rows.astype(jnp.float32), carry_state, precision=lax.Precision.HIGHEST)
    carried = carried * jnp.exp(cumlog).T[:, :, None]
    last_log = cumlog[:, -1]
    weighted_values = (key_matrix_rows.astype(jnp.float32) * jnp.exp(last_log[:, None] - cumlog).T[:, :, None]).astype(jnp.bfloat16)
    state_update = jnp.einsum('jxa,jxp->xap', weighted_values.astype(jnp.float32), value_rows.astype(jnp.float32))
    carry_state = jnp.exp(last_log)[:, None, None] * carry_state + state_update
    return carry_state, (within + carried).astype(jnp.bfloat16)


def section_step(carry_state, section_pair):
    carry_state, retained = lax.scan(block_step, carry_state, section_pair)
    return carry_state, (retained, carry_state)


def reference(q_prompt, k_prompt, v_prompt, log_decay, prompt_section, q_step, k_step, v_step, step_decay, w_out):
    block_count = TOK_DEV // BLOCK

    def reshaped(array):
        return array.reshape(N_CTX, block_count, BLOCK, RETENTION_HEADS, HD)

    log_blocks = log_decay.reshape(RETENTION_HEADS, N_CTX, block_count, BLOCK).transpose(1, 2, 0, 3)
    zero_state = jnp.zeros((RETENTION_HEADS, HD, HD), jnp.float32)
    ignored, (retained, boundaries) = lax.scan(
        section_step, zero_state, (reshaped(q_prompt), reshaped(k_prompt), reshaped(v_prompt), log_blocks))
    retention = retained.reshape(PROMPT_TOKENS, RETENTION_HEADS * HD)
    prompt_out = jnp.dot(retention, w_out, preferred_element_type=jnp.float32).astype(jnp.bfloat16)

    section_ids = prompt_section[:, 0]
    step_queries = q_step.astype(jnp.float32)

    def read_one(running, section_pair):
        section_index, boundary = section_pair
        selector = (section_ids == section_index).astype(jnp.float32)
        reads = jnp.einsum('rthd,hde->rthe', step_queries, boundary, precision=lax.Precision.HIGHEST)
        return running + selector[:, None, None, None] * reads, None

    prefix_reads, ignored_too = lax.scan(
        read_one, jnp.zeros((ROWS, STEPS, RETENTION_HEADS, HD), jnp.float32),
        (jnp.arange(N_CTX, dtype=jnp.int32), boundaries))
    step_logs = jnp.cumsum(jnp.transpose(step_decay, (2, 1, 0)), axis=1)
    head_logs = jnp.transpose(step_logs, (0, 2, 1))
    step_index = jnp.arange(STEPS)
    causal = step_index[:, None] >= step_index[None, :]
    step_weights = jnp.where(causal[None, None], jnp.exp(jnp.minimum(head_logs[:, :, :, None] - head_logs[:, :, None, :], 0.0)), 0.0)
    attention_scores = jnp.einsum('rthd,ruhd->rhtu', step_queries, k_step.astype(jnp.float32))
    own_terms = jnp.einsum('rhtu,ruhe->rthe', attention_scores * step_weights, v_step.astype(jnp.float32))
    step_retention = (jnp.exp(step_logs)[:, :, :, None] * prefix_reads + own_terms).astype(jnp.bfloat16)
    step_flat = step_retention.reshape(ROWS * STEPS, RETENTION_HEADS * HD)
    step_out = jnp.dot(step_flat, w_out, preferred_element_type=jnp.float32).astype(jnp.bfloat16)
    return prompt_out, step_out.reshape(ROWS, STEPS, D)
```

```python
import functools
import jax
import jax.numpy as jnp
from jax import lax
from jax.experimental import pallas as pl
from jax.experimental.pallas import tpu as pltpu
from jax.sharding import PartitionSpec as P

CAP = 4
MESH = pl.DeviceIdType.MESH
F32 = jnp.float32
BF16 = jnp.bfloat16


def mm(a, b):
    return jnp.dot(a, b, preferred_element_type=F32)


def retention_kernel(
    sections,
    q_ref, k_ref, v_ref, cum_ref, cum_t_ref, total_ref,
    qs_ref, ks_ref, vs_ref, step_log_ref, pack_ref, unpack_ref,
    out_ref,
    state_out, query_out, state_in, query_in, total_in,
    boundary, entry_out, read_out, entry_in, read_in, within, own,
    send_s, send_a, send_q, send_e, send_r,
    recv_s, recv_a, recv_q, recv_e, recv_r,
):
    me = lax.axis_index("ctx")
    heads = total_ref.shape[0]
    tokens = q_ref.shape[0]
    hd = q_ref.shape[1] // heads
    rows = step_log_ref.shape[0]
    steps = qs_ref.shape[0] // rows

    def peer(d):
        return lax.rem(me + d, sections)

    def push(src, dst, send, recv, to):
        return pltpu.make_async_remote_copy(
            src_ref=src, dst_ref=dst, send_sem=send, recv_sem=recv,
            device_id={"ctx": to}, device_id_type=MESH,
        )

    barrier = pltpu.get_barrier_semaphore()
    for d in range(1, sections):
        pl.semaphore_signal(barrier, inc=1, device_id={"ctx": peer(d)}, device_id_type=MESH)

    def lanes(h):
        return slice(h * hd, (h + 1) * hd)

    for h in range(heads):
        column = cum_t_ref[:, h:h + 1]
        keys = (k_ref[:, lanes(h)].astype(F32) * jnp.exp(total_ref[h, 0:1, 0:1] - column)).astype(BF16)
        state_out[h] = lax.dot_general(
            keys, v_ref[:, lanes(h)], (((0,), (0,)), ((), ())), preferred_element_type=F32
        ).astype(BF16)
    pl.semaphore_wait(barrier, sections - 1)
    for d in range(1, sections):
        to = peer(d)
        push(total_ref.at[to], total_in.at[me], send_a.at[d], recv_a.at[me], to).start()
        push(state_out.at[to], state_in.at[me], send_s.at[d], recv_s.at[me], to).start()
    state_in[me] = state_out[me]
    total_in[me] = total_ref[me]
    for h in range(heads):
        query_out[h] = mm(pack_ref[...], qs_ref[:, lanes(h)]).astype(BF16)
    for d in range(1, sections):
        to = peer(d)
        push(query_out.at[to], query_in.at[me], send_q.at[d], recv_q.at[me], to).start()
    query_in[me] = query_out[me]

    causal = (
        lax.broadcasted_iota(jnp.int32, (tokens, tokens), 0)
        >= lax.broadcasted_iota(jnp.int32, (tokens, tokens), 1)
    )
    for h in range(heads):
        scores = lax.dot_general(
            q_ref[:, lanes(h)], k_ref[:, lanes(h)], (((1,), (1,)), ((), ())),
            preferred_element_type=F32,
        )
        gap = jnp.minimum(cum_t_ref[:, h:h + 1] - cum_ref[h:h + 1, :], 0.0)
        weights = jnp.where(causal, scores * jnp.exp(gap), 0.0).astype(BF16)
        within[:, lanes(h)] = mm(weights, v_ref[:, lanes(h)])

    for h in range(heads):
        for t in range(steps):
            here = slice(t * rows, (t + 1) * rows)
            query = qs_ref[here, lanes(h)].astype(F32)
            log_t = step_log_ref[:, t * heads + h:t * heads + h + 1]
            acc = jnp.zeros((rows, hd), F32)
            for u in range(t + 1):
                there = slice(u * rows, (u + 1) * rows)
                score = jnp.sum(query * ks_ref[there, lanes(h)].astype(F32), axis=1, keepdims=True)
                log_u = step_log_ref[:, u * heads + h:u * heads + h + 1]
                weight = score * jnp.exp(jnp.minimum(log_t - log_u, 0.0))
                acc = acc + weight * vs_ref[there, lanes(h)].astype(F32)
            own[here, lanes(h)] = acc

    for d in range(1, sections):
        frm = peer(d)
        push(total_ref.at[frm], total_in.at[frm], send_a.at[d], recv_a.at[frm], frm).wait_recv()
        push(state_out.at[frm], state_in.at[frm], send_s.at[d], recv_s.at[frm], frm).wait_recv()
    state = jnp.zeros((hd, hd), F32)
    for c in range(sections):
        entry_out[c] = state.astype(BF16)
        state = jnp.exp(total_in[c, 0:1, 0:1]) * state + state_in[c].astype(F32)
        boundary[c] = state.astype(BF16)
    for d in range(1, sections):
        to = peer(d)
        push(entry_out.at[to], entry_in.at[me], send_e.at[d], recv_e.at[me], to).start()
    entry_in[me] = entry_out[me]

    for d in range(1, sections):
        frm = peer(d)
        push(query_out.at[frm], query_in.at[frm], send_q.at[d], recv_q.at[frm], frm).wait_recv()
    span = CAP * steps
    for c in range(sections):
        part = slice(c * span, (c + 1) * span)
        asked = query_in[:, part, :].reshape(sections * span, hd)
        read_out[:, part, :] = mm(asked, boundary[c]).astype(BF16).reshape(sections, span, hd)
    for d in range(1, sections):
        to = peer(d)
        push(read_out.at[to], read_in.at[me], send_r.at[d], recv_r.at[me], to).start()
    read_in[me] = read_out[me]

    for d in range(1, sections):
        frm = peer(d)
        push(entry_out.at[frm], entry_in.at[frm], send_e.at[d], recv_e.at[frm], frm).wait_recv()
    for h in range(heads):
        carried = mm(q_ref[:, lanes(h)], entry_in[h]) * jnp.exp(cum_t_ref[:, h:h + 1])
        out_ref[0:tokens, lanes(h)] = (within[:, lanes(h)] + carried).astype(BF16)

    for d in range(1, sections):
        frm = peer(d)
        push(read_out.at[frm], read_in.at[frm], send_r.at[d], recv_r.at[frm], frm).wait_recv()
    for h in range(heads):
        reads = mm(unpack_ref[...], read_in[h])
        for t in range(steps):
            here = slice(t * rows, (t + 1) * rows)
            grown = jnp.exp(step_log_ref[:, t * heads + h:t * heads + h + 1])
            out_ref[tokens + t * rows:tokens + (t + 1) * rows, lanes(h)] = (
                grown * reads[here] + own[here, lanes(h)]
            ).astype(BF16)

    for d in range(1, sections):
        to = peer(d)
        push(total_ref.at[to], total_in.at[me], send_a.at[d], recv_a.at[me], to).wait_send()
        push(state_out.at[to], state_in.at[me], send_s.at[d], recv_s.at[me], to).wait_send()
        push(query_out.at[to], query_in.at[me], send_q.at[d], recv_q.at[me], to).wait_send()
        push(entry_out.at[to], entry_in.at[me], send_e.at[d], recv_e.at[me], to).wait_send()
        push(read_out.at[to], read_in.at[me], send_r.at[d], recv_r.at[me], to).wait_send()


def project_kernel(
    n, r_ref, w_ref, out_ref, gathered, weights, total, load_sem, send_sem, recv_sem
):
    at = lax.axis_index("head")
    chunks, _, depth = r_ref.shape
    columns = w_ref.shape[1]
    tile = min(columns, 512)

    def load(j):
        return pltpu.make_async_copy(
            w_ref.at[pl.ds(pl.multiple_of(j * depth, depth), depth)], weights.at[j], load_sem.at[j]
        )

    def push(src, j, m, way, s):
        return pltpu.make_async_remote_copy(
            src_ref=src, dst_ref=gathered.at[j, m],
            send_sem=send_sem.at[way, s, m], recv_sem=recv_sem.at[j, m],
            device_id={"head": at + 1 if way == 0 else at - 1}, device_id_type=MESH,
        )

    has_left, has_right = at > 0, at < n - 1
    barrier = pltpu.get_barrier_semaphore()

    @pl.when(has_left)
    def _():
        pl.semaphore_signal(barrier, inc=1, device_id={"head": at - 1}, device_id_type=MESH)

    @pl.when(has_right)
    def _():
        pl.semaphore_signal(barrier, inc=1, device_id={"head": at + 1}, device_id_type=MESH)

    pl.semaphore_wait(barrier, has_left.astype(jnp.int32) + has_right.astype(jnp.int32))

    for m in range(chunks):
        @pl.when(has_right)
        def _():
            push(r_ref.at[m], at, m, 0, 0).start()

        @pl.when(has_left)
        def _():
            push(r_ref.at[m], at, m, 1, 0).start()

    for j in range(n):
        load(j).start()

    def multiply(rows, j, m, first):
        def body(i, carry):
            cols = pl.ds(pl.multiple_of(i * tile, tile), tile)
            term = mm(rows[...], weights[j, :, cols])
            if first:
                total[m, :, cols] = term
            else:
                total[m, :, cols] += term
            return carry

        lax.fori_loop(0, columns // tile, body, 0)

    for j in range(n):
        load(j).wait()

    def own_step(m, carry):
        multiply(r_ref.at[m], at, m, True)
        return carry

    lax.fori_loop(0, chunks, own_step, 0)

    def step(i, carry):
        s, m = i // chunks + 1, lax.rem(i, chunks)
        low, high = at - s, at + s

        @pl.when(low >= 0)
        def _():
            push(gathered.at[low, m], low, m, 0, s).wait_recv()

            @pl.when(has_right)
            def _():
                push(gathered.at[low, m], low, m, 0, s).start()

        @pl.when(high < n)
        def _():
            push(gathered.at[high, m], high, m, 1, s).wait_recv()

            @pl.when(has_left)
            def _():
                push(gathered.at[high, m], high, m, 1, s).start()

        @pl.when(low >= 0)
        def _():
            multiply(gathered.at[low, m], low, m, False)

        @pl.when(high < n)
        def _():
            multiply(gathered.at[high, m], high, m, False)

        return carry

    lax.fori_loop(0, (n - 1) * chunks, step, 0)

    def finish(m, carry):
        out_ref[m] = total[m].astype(BF16)
        return carry

    lax.fori_loop(0, chunks, finish, 0)

    def drain(i, carry):
        s, m = i // chunks, lax.rem(i, chunks)

        @pl.when((at - s >= 0) & has_right)
        def _():
            push(r_ref.at[m], at - s, m, 0, s).wait_send()

        @pl.when((at + s < n) & has_left)
        def _():
            push(r_ref.at[m], at + s, m, 1, s).wait_send()

        return carry

    lax.fori_loop(0, n * chunks, drain, 0)


def project(flat, w_out):
    n = lax.axis_size("head")
    chunk = 128
    chunks, depth = flat.shape[0] // chunk, flat.shape[1]
    columns = w_out.shape[1]
    vmem = pl.BlockSpec(memory_space=pltpu.VMEM)
    out = pl.pallas_call(
        functools.partial(project_kernel, n),
        out_shape=jax.ShapeDtypeStruct((chunks, chunk, columns), BF16),
        in_specs=[vmem, pl.BlockSpec(memory_space=pl.ANY)],
        out_specs=vmem,
        scratch_shapes=[
            pltpu.VMEM((n, chunks, chunk, depth), BF16),
            pltpu.VMEM((n, depth, columns), BF16),
            pltpu.VMEM((chunks, chunk, columns), F32),
            pltpu.SemaphoreType.DMA((n,)),
            pltpu.SemaphoreType.DMA((2, n, chunks)),
            pltpu.SemaphoreType.DMA((n, chunks)),
        ],
        compiler_params=pltpu.CompilerParams(
            collective_id=1, has_side_effects=True, vmem_limit_bytes=60 * 2**20
        ),
        name="project",
    )(flat.reshape(chunks, chunk, depth), w_out)
    return out.reshape(chunks * chunk, columns)


def retain(q, k, v, log_decay, prompt_section, q_step, k_step, v_step, step_decay):
    tokens, heads, hd = q.shape
    rows, steps = q_step.shape[:2]
    sections = lax.axis_size("ctx")
    cumlog = jnp.cumsum(log_decay, axis=1)
    totals = jnp.broadcast_to(cumlog[:, -1][:, None, None], (heads, 8, 128))
    section_ids = prompt_section[:, 0]
    same = section_ids[:, None] == section_ids[None, :]
    ranking = jnp.sum(jnp.where(jnp.tril(same, -1), 1, 0), axis=1)
    slot = (jnp.arange(sections)[:, None, None] * CAP + jnp.arange(CAP)[None, None, :])
    slot = jnp.broadcast_to(slot, (sections, steps, CAP)).reshape(-1)
    slot_step = jnp.broadcast_to(jnp.arange(steps)[None, :, None], (sections, steps, CAP)).reshape(-1)
    row_slot = jnp.tile(section_ids * CAP + ranking, steps)
    row_step = jnp.repeat(jnp.arange(steps), rows)
    pack = (slot[:, None] == row_slot[None, :]) & (slot_step[:, None] == row_step[None, :])
    unpack = (row_slot[:, None] == slot[None, :]) & (row_step[:, None] == slot_step[None, :])
    step_logs = jnp.cumsum(step_decay, axis=1)
    step_logs = jnp.transpose(step_logs, (2, 1, 0)).reshape(rows, steps * heads)

    def wide(a):
        return a.reshape(tokens, heads * hd)

    def by_step(a):
        return jnp.transpose(a, (1, 0, 2, 3)).reshape(steps * rows, heads * hd)

    vmem = pl.BlockSpec(memory_space=pltpu.VMEM)
    count = sections * CAP * steps
    state = pltpu.VMEM((sections, hd, hd), BF16)
    reads = pltpu.VMEM((sections, count, hd), BF16)
    return pl.pallas_call(
        functools.partial(retention_kernel, sections),
        out_shape=jax.ShapeDtypeStruct((tokens + rows * steps, heads * hd), BF16),
        in_specs=[vmem] * 12,
        out_specs=vmem,
        scratch_shapes=[
            state, reads, state, reads, pltpu.VMEM((sections, 8, 128), F32),
            state, state, reads, state, reads,
            pltpu.VMEM((tokens, heads * hd), F32),
            pltpu.VMEM((rows * steps, heads * hd), F32),
        ] + [pltpu.SemaphoreType.DMA((sections,))] * 10,
        compiler_params=pltpu.CompilerParams(
            collective_id=0, has_side_effects=True, vmem_limit_bytes=48 * 2**20
        ),
        name="retain",
    )(
        wide(q), wide(k), wide(v), cumlog, cumlog.T, totals,
        by_step(q_step), by_step(k_step), by_step(v_step), step_logs,
        pack.astype(BF16), unpack.astype(BF16),
    )


def entering(value, axis, join, neutral):
    count, mine = (lax.axis_size(axis), lax.axis_index(axis))
    pieces = jax.tree.map(lambda part: lax.all_gather(part, axis), value)
    running = jax.tree.map(
        lambda part, zero: jnp.full_like(part, 0) + jnp.asarray(zero, part.dtype), value, neutral
    )

    def step(position, running):
        longer = join(running, jax.tree.map(lambda part: part[position], pieces))
        return jax.tree.map(lambda new, old: jnp.where(position < mine, new, old), longer, running)

    return lax.fori_loop(0, count - 1, step, running)


def as_sent(value):
    return jax.tree.map(lambda a: a.astype(jnp.bfloat16) if a.dtype == jnp.float32 else a, value)


def split_state(state):
    high_part = state.astype(jnp.bfloat16)
    rest = state - lax.optimization_barrier(high_part).astype(jnp.float32)
    middle_part = rest.astype(jnp.bfloat16)
    low_part = (rest - lax.optimization_barrier(middle_part).astype(jnp.float32)).astype(
        jnp.bfloat16
    )
    return (high_part, middle_part, low_part)


def exact_read(form, query_rows, state):
    parts = split_state(state)
    total = jnp.einsum(form, query_rows, parts[0], preferred_element_type=jnp.float32)
    total = total + jnp.einsum(form, query_rows, parts[1], preferred_element_type=jnp.float32)
    return total + jnp.einsum(form, query_rows, parts[2], preferred_element_type=jnp.float32)


def block_terms(carry_state, query_rows, key_matrix_rows, value_rows, log_rates):
    positions = jnp.arange(log_rates.shape[1])
    causal = positions[:, None] >= positions[None, :]
    cumlog = jnp.cumsum(log_rates, axis=1)
    decays = jnp.where(
        causal[None], jnp.exp(jnp.minimum(cumlog[:, :, None] - cumlog[:, None, :], 0.0)), 0.0
    )
    attention_scores = jnp.einsum(
        "jsv,csv->sjc", query_rows, key_matrix_rows, preferred_element_type=jnp.float32
    )
    weights = (attention_scores * decays).astype(jnp.bfloat16)
    within = jnp.einsum("hnm,mhe->nhe", weights, value_rows, preferred_element_type=jnp.float32)
    carried = exact_read("nhd,hde->nhe", query_rows, carry_state)
    carried = carried * jnp.exp(cumlog).T[:, :, None]
    last_log = cumlog[:, -1]
    weighted_values = (
        key_matrix_rows.astype(jnp.float32) * jnp.exp(last_log[:, None] - cumlog).T[:, :, None]
    ).astype(jnp.bfloat16)
    state_update = jnp.einsum(
        "jxa,jxp->xap", weighted_values, value_rows, preferred_element_type=jnp.float32
    )
    carry_state = jnp.exp(last_log)[:, None, None] * carry_state + state_update
    return (carry_state, within + carried, cumlog)


def combine(earlier, latter):
    return (earlier[0] + latter[0], jnp.exp(latter[0])[:, None, None] * earlier[1] + latter[1])


def retain_gathered(
    q_prompt, k_prompt, v_prompt, log_decay, prompt_section, q_step, k_step, v_step, step_decay
):
    token_count, heads_here, head_dim = q_prompt.shape
    sections = lax.axis_size("ctx")
    carry_state = jnp.zeros((heads_here, head_dim, head_dim), jnp.float32)
    carry_state, partial_value, cumlog = block_terms(
        carry_state, q_prompt, k_prompt, v_prompt, log_decay
    )
    offset = cumlog[:, -1]
    identity = (jnp.zeros_like(offset), jnp.zeros_like(carry_state))
    earlier_log, entry_state = entering((offset, carry_state), "ctx", combine, identity)
    entry_parts = split_state(entry_state)
    entry_read = jnp.einsum(
        "nhd,hde->nhe", q_prompt, entry_parts[0], preferred_element_type=jnp.float32
    )
    entry_read = entry_read + jnp.einsum(
        "nhd,hde->nhe", q_prompt, entry_parts[1], preferred_element_type=jnp.float32
    )
    entry_read = entry_read + jnp.einsum(
        "nhd,hde->nhe", q_prompt, entry_parts[2], preferred_element_type=jnp.float32
    )
    block_out = partial_value + jnp.exp(cumlog).T[:, :, None] * entry_read
    retained = block_out.astype(jnp.bfloat16)
    retention = retained.reshape(token_count, heads_here * head_dim)

    final_state = jnp.exp(offset)[:, None, None] * entry_state + carry_state
    row_count, step_count = (q_step.shape[0], q_step.shape[1])
    section_ids = prompt_section[:, 0]
    owner_hot = (section_ids[:, None] == jnp.arange(sections)[None, :]).astype(jnp.float32)
    before = jnp.tril(jnp.ones((row_count, row_count), jnp.float32), -1)
    counts_before = jnp.dot(before, owner_hot, precision=lax.Precision.HIGHEST)
    ranking = jnp.sum(counts_before * owner_hot, axis=1).astype(jnp.int32)
    slot_ids = section_ids * CAP + ranking
    selector = (jnp.arange(sections * CAP)[:, None] == slot_ids[None, :]).astype(jnp.bfloat16)
    packed = jnp.dot(selector, q_step.reshape(row_count, -1), preferred_element_type=jnp.float32)
    packed = packed.astype(jnp.bfloat16).reshape(sections, CAP, step_count, heads_here, head_dim)
    reads = exact_read(
        "jcthd,jhde->jcthe",
        packed,
        lax.all_gather(as_sent(final_state[None]), "ctx", axis=0, tiled=True),
    )
    slot_reads = reads
    slot_reads = slot_reads.reshape(sections * CAP, step_count, heads_here, head_dim)
    prefix_reads = jnp.take(slot_reads, slot_ids, axis=0)
    step_logs = jnp.cumsum(jnp.transpose(step_decay, (2, 1, 0)), axis=1)
    head_logs = jnp.transpose(step_logs, (0, 2, 1))
    step_index = jnp.arange(step_count)
    causal = step_index[:, None] >= step_index[None, :]
    step_weights = jnp.where(
        causal[None, None],
        jnp.exp(jnp.minimum(head_logs[:, :, :, None] - head_logs[:, :, None, :], 0.0)),
        0.0,
    )
    attention_scores = jnp.einsum(
        "rthd,ruhd->rhtu", q_step, k_step, preferred_element_type=jnp.float32
    )
    own_terms = jnp.einsum(
        "rhtu,ruhe->rthe", attention_scores * step_weights, v_step.astype(jnp.float32)
    )
    step_retention = (jnp.exp(step_logs)[:, :, :, None] * prefix_reads + own_terms).astype(
        jnp.bfloat16
    )
    step_flat = jnp.transpose(step_retention, (1, 0, 2, 3))
    step_flat = step_flat.reshape(row_count * step_count, heads_here * head_dim)
    return jnp.concatenate([retention, step_flat], axis=0)


def shards(
    q_prompt,
    k_prompt,
    v_prompt,
    log_decay,
    prompt_section,
    q_step,
    k_step,
    v_step,
    step_decay,
    w_out,
):
    tokens, heads = q_prompt.shape[:2]
    rows, steps = q_step.shape[:2]
    form = retain if heads == lax.axis_size("ctx") else retain_gathered
    flat = form(
        q_prompt, k_prompt, v_prompt, log_decay, prompt_section, q_step, k_step, v_step, step_decay
    )
    out = project(flat, w_out)
    step_out = out[tokens:].reshape(steps, rows, w_out.shape[1])
    return (out[:tokens], jnp.transpose(step_out, (1, 0, 2)))


def solution(mesh):
    in_specs = (
        P("ctx", "head", None),
        P("ctx", "head", None),
        P("ctx", "head", None),
        P("head", "ctx"),
        P("ctx", None),
        P("ctx", None, "head", None),
        P("ctx", None, "head", None),
        P("ctx", None, "head", None),
        P("head", None, "ctx"),
        P(None, "head"),
    )
    out_specs = (P("ctx", "head"), P("ctx", None, "head"))
    return jax.shard_map(shards, mesh=mesh, in_specs=in_specs, out_specs=out_specs, check_vma=False)
```

```python
import functools
import jax
import jax.numpy as jnp
from jax import lax
from jax.experimental import pallas as pl
from jax.experimental.pallas import tpu as pltpu
from jax.sharding import PartitionSpec as P

CAP = 4
MESH = pl.DeviceIdType.MESH
F32 = jnp.float32
BF16 = jnp.bfloat16


def mm(a, b):
    return jnp.dot(a, b, preferred_element_type=F32)


def fused_kernel(
    sections,
    q_ref, k_ref, v_ref, cum_ref, cum_t_ref, total_ref,
    qs_ref, ks_ref, vs_ref, step_log_ref, pack_ref, unpack_ref,
    w_ref,
    prompt_ref, step_ref,
    state_out, query_out, state_in, query_in, total_in,
    boundary, entry_out, read_out, entry_in, read_in, gathered, weights, total,
    send_s, send_a, send_q, send_e, send_r,
    recv_s, recv_a, recv_q, recv_e, recv_r,
    load_sem, send_z, recv_z,
):
    me = lax.axis_index("ctx")
    at = lax.axis_index("head")
    n = lax.axis_size("head")
    has_left, has_right = at > 0, at < n - 1
    chunks, chunk, depth = total.shape
    parts = chunks - 1
    tile = 512
    far = jnp.where(at < 2, 3, 0)
    near = jnp.where(at == 1, 0, 1)

    def slot_of(j):
        return jnp.where((j == at) | (j == far), 0, jnp.where(j == near, 1, 2))

    def load(j, sem):
        return pltpu.make_async_copy(
            w_ref.at[pl.ds(pl.multiple_of(j * depth, depth), depth)],
            weights.at[slot_of(j)], load_sem.at[sem],
        )

    def pass_on(j, m, way, s):
        return pltpu.make_async_remote_copy(
            src_ref=gathered.at[j, m], dst_ref=gathered.at[j, m],
            send_sem=send_z.at[way, s, m], recv_sem=recv_z.at[j, m],
            device_id={"head": at + 1 if way == 0 else at - 1}, device_id_type=MESH,
        )

    def send_own(m):
        @pl.when(has_right)
        def _():
            pass_on(at, m, 0, 0).start()

        @pl.when(has_left)
        def _():
            pass_on(at, m, 1, 0).start()
    heads = total_ref.shape[0]
    tokens = q_ref.shape[0]
    hd = q_ref.shape[1] // heads
    rows = step_log_ref.shape[0]
    steps = qs_ref.shape[0] // rows

    def peer(d):
        return lax.rem(me + d, sections)

    def push(src, dst, send, recv, to):
        return pltpu.make_async_remote_copy(
            src_ref=src, dst_ref=dst, send_sem=send, recv_sem=recv,
            device_id={"ctx": to}, device_id_type=MESH,
        )

    barrier = pltpu.get_barrier_semaphore()
    for d in range(1, sections):
        pl.semaphore_signal(barrier, inc=1, device_id={"ctx": peer(d)}, device_id_type=MESH)

    @pl.when(has_left)
    def _():
        pl.semaphore_signal(barrier, inc=1, device_id={"head": at - 1}, device_id_type=MESH)

    @pl.when(has_right)
    def _():
        pl.semaphore_signal(barrier, inc=1, device_id={"head": at + 1}, device_id_type=MESH)

    other = jnp.where(at == 1, 2, jnp.where(at == 2, 3, 2))
    load(at, 0).start()
    load(near, 1).start()
    load(other, 2).start()

    def lanes(h):
        return slice(h * hd, (h + 1) * hd)

    for h in range(heads):
        column = cum_t_ref[:, h:h + 1]
        keys = (k_ref[:, lanes(h)].astype(F32) * jnp.exp(total_ref[h, 0:1, 0:1] - column)).astype(BF16)
        state_out[h] = lax.dot_general(
            keys, v_ref[:, lanes(h)], (((0,), (0,)), ((), ())), preferred_element_type=F32
        ).astype(BF16)
    pl.semaphore_wait(
        barrier, sections - 1 + has_left.astype(jnp.int32) + has_right.astype(jnp.int32)
    )
    for d in range(1, sections):
        to = peer(d)
        push(total_ref.at[to], total_in.at[me], send_a.at[d], recv_a.at[me], to).start()
        push(state_out.at[to], state_in.at[me], send_s.at[d], recv_s.at[me], to).start()
    state_in[me] = state_out[me]
    total_in[me] = total_ref[me]
    for h in range(heads):
        query_out[h] = mm(pack_ref[...], qs_ref[:, lanes(h)]).astype(BF16)
    for d in range(1, sections):
        to = peer(d)
        push(query_out.at[to], query_in.at[me], send_q.at[d], recv_q.at[me], to).start()
    query_in[me] = query_out[me]

    causal = (
        lax.broadcasted_iota(jnp.int32, (tokens, tokens), 0)
        >= lax.broadcasted_iota(jnp.int32, (tokens, tokens), 1)
    )
    for h in range(heads):
        scores = lax.dot_general(
            q_ref[:, lanes(h)], k_ref[:, lanes(h)], (((1,), (1,)), ((), ())),
            preferred_element_type=F32,
        )
        gap = jnp.minimum(cum_t_ref[:, h:h + 1] - cum_ref[h:h + 1, :], 0.0)
        scaled = jnp.where(causal, scores * jnp.exp(gap), 0.0).astype(BF16)
        total[0:parts, :, lanes(h)] = mm(scaled, v_ref[:, lanes(h)]).reshape(parts, chunk, hd)

    for d in range(1, sections):
        frm = peer(d)
        push(total_ref.at[frm], total_in.at[frm], send_a.at[d], recv_a.at[frm], frm).wait_recv()
        push(state_out.at[frm], state_in.at[frm], send_s.at[d], recv_s.at[frm], frm).wait_recv()
    state = jnp.zeros((hd, hd), F32)
    for c in range(sections):
        entry_out[c] = state.astype(BF16)
        state = jnp.exp(total_in[c, 0:1, 0:1]) * state + state_in[c].astype(F32)
        boundary[c] = state.astype(BF16)
    for d in range(1, sections):
        to = peer(d)
        push(entry_out.at[to], entry_in.at[me], send_e.at[d], recv_e.at[me], to).start()
    entry_in[me] = entry_out[me]

    for d in range(1, sections):
        frm = peer(d)
        push(query_out.at[frm], query_in.at[frm], send_q.at[d], recv_q.at[frm], frm).wait_recv()
    span = CAP * steps
    for c in range(sections):
        part = slice(c * span, (c + 1) * span)
        asked = query_in[:, part, :].reshape(sections * span, hd)
        read_out[:, part, :] = mm(asked, boundary[c]).astype(BF16).reshape(sections, span, hd)
    for d in range(1, sections):
        to = peer(d)
        push(read_out.at[to], read_in.at[me], send_r.at[d], recv_r.at[me], to).start()
    read_in[me] = read_out[me]

    for h in range(heads):
        for t in range(steps):
            here = slice(t * rows, (t + 1) * rows)
            query = qs_ref[here, lanes(h)].astype(F32)
            log_t = step_log_ref[:, t * heads + h:t * heads + h + 1]
            acc = jnp.zeros((rows, hd), F32)
            for u in range(t + 1):
                there = slice(u * rows, (u + 1) * rows)
                score = jnp.sum(query * ks_ref[there, lanes(h)].astype(F32), axis=1, keepdims=True)
                log_u = step_log_ref[:, u * heads + h:u * heads + h + 1]
                weight = score * jnp.exp(jnp.minimum(log_t - log_u, 0.0))
                acc = acc + weight * vs_ref[there, lanes(h)].astype(F32)
            total[parts, here, lanes(h)] = acc

    for d in range(1, sections):
        frm = peer(d)
        push(entry_out.at[frm], entry_in.at[frm], send_e.at[d], recv_e.at[frm], frm).wait_recv()
    for m in range(parts):
        here = slice(m * chunk, (m + 1) * chunk)
        for h in range(heads):
            carried = mm(q_ref[here, lanes(h)], entry_in[h]) * jnp.exp(cum_t_ref[here, h:h + 1])
            gathered[at, m, :, lanes(h)] = (total[m, :, lanes(h)] + carried).astype(BF16)
        send_own(m)

    for d in range(1, sections):
        frm = peer(d)
        push(read_out.at[frm], read_in.at[frm], send_r.at[d], recv_r.at[frm], frm).wait_recv()
    for h in range(heads):
        reads = mm(unpack_ref[...], read_in[h])
        for t in range(steps):
            here = slice(t * rows, (t + 1) * rows)
            grown = jnp.exp(step_log_ref[:, t * heads + h:t * heads + h + 1])
            gathered[at, parts, here, lanes(h)] = (
                grown * reads[here] + total[parts, here, lanes(h)]
            ).astype(BF16)
    send_own(parts)

    def multiply(j, m, first):
        slot = slot_of(j)

        def body(i, carry):
            cols = pl.ds(pl.multiple_of(i * tile, tile), tile)
            term = mm(gathered[j, m], weights[slot, :, cols])
            if first:
                total[m, :, cols] = term
                return carry

            @pl.when(j != far)
            def _():
                total[m, :, cols] += term

            @pl.when((j == far) & (m < parts))
            def _():
                here = pl.ds(pl.multiple_of(jnp.minimum(m, parts - 1) * chunk, chunk), chunk)
                prompt_ref[here, cols] = (total[m, :, cols] + term).astype(BF16)

            @pl.when((j == far) & (m == parts))
            def _():
                step_ref[:, cols] = (total[m, :, cols] + term).astype(BF16)

            return carry

        lax.fori_loop(0, depth // tile, body, 0)

    load(at, 0).wait()

    def own_step(m, carry):
        multiply(at, m, True)
        return carry

    lax.fori_loop(0, chunks, own_step, 0)
    load(far, 3).start()
    load(near, 1).wait()
    load(other, 2).wait()
    load(far, 3).wait()

    def step(i, carry):
        s, m = i // chunks + 1, lax.rem(i, chunks)
        low, high = at - s, at + s

        @pl.when(low >= 0)
        def _():
            pass_on(low, m, 0, s).wait_recv()

            @pl.when(has_right)
            def _():
                pass_on(low, m, 0, s).start()

        @pl.when(high < n)
        def _():
            pass_on(high, m, 1, s).wait_recv()

            @pl.when(has_left)
            def _():
                pass_on(high, m, 1, s).start()

        @pl.when(low >= 0)
        def _():
            multiply(low, m, False)

        @pl.when(high < n)
        def _():
            multiply(high, m, False)

        return carry

    lax.fori_loop(0, (n - 1) * chunks, step, 0)

    def drain(i, carry):
        s, m = i // chunks, lax.rem(i, chunks)

        @pl.when((at - s >= 0) & has_right)
        def _():
            pass_on(at - s, m, 0, s).wait_send()

        @pl.when((at + s < n) & has_left)
        def _():
            pass_on(at + s, m, 1, s).wait_send()

        return carry

    lax.fori_loop(0, n * chunks, drain, 0)

    for d in range(1, sections):
        to = peer(d)
        push(total_ref.at[to], total_in.at[me], send_a.at[d], recv_a.at[me], to).wait_send()
        push(state_out.at[to], state_in.at[me], send_s.at[d], recv_s.at[me], to).wait_send()
        push(query_out.at[to], query_in.at[me], send_q.at[d], recv_q.at[me], to).wait_send()
        push(entry_out.at[to], entry_in.at[me], send_e.at[d], recv_e.at[me], to).wait_send()
        push(read_out.at[to], read_in.at[me], send_r.at[d], recv_r.at[me], to).wait_send()


def project_kernel(
    n, r_ref, w_ref, out_ref, gathered, weights, total, load_sem, send_sem, recv_sem
):
    at = lax.axis_index("head")
    chunks, _, depth = r_ref.shape
    columns = w_ref.shape[1]
    tile = min(columns, 512)

    def load(j):
        return pltpu.make_async_copy(
            w_ref.at[pl.ds(pl.multiple_of(j * depth, depth), depth)], weights.at[j], load_sem.at[j]
        )

    def push(src, j, m, way, s):
        return pltpu.make_async_remote_copy(
            src_ref=src, dst_ref=gathered.at[j, m],
            send_sem=send_sem.at[way, s, m], recv_sem=recv_sem.at[j, m],
            device_id={"head": at + 1 if way == 0 else at - 1}, device_id_type=MESH,
        )

    has_left, has_right = at > 0, at < n - 1
    barrier = pltpu.get_barrier_semaphore()

    @pl.when(has_left)
    def _():
        pl.semaphore_signal(barrier, inc=1, device_id={"head": at - 1}, device_id_type=MESH)

    @pl.when(has_right)
    def _():
        pl.semaphore_signal(barrier, inc=1, device_id={"head": at + 1}, device_id_type=MESH)

    pl.semaphore_wait(barrier, has_left.astype(jnp.int32) + has_right.astype(jnp.int32))

    for m in range(chunks):
        @pl.when(has_right)
        def _():
            push(r_ref.at[m], at, m, 0, 0).start()

        @pl.when(has_left)
        def _():
            push(r_ref.at[m], at, m, 1, 0).start()

    for j in range(n):
        load(j).start()

    def multiply(rows, j, m, first):
        def body(i, carry):
            cols = pl.ds(pl.multiple_of(i * tile, tile), tile)
            term = mm(rows[...], weights[j, :, cols])
            if first:
                total[m, :, cols] = term
            else:
                total[m, :, cols] += term
            return carry

        lax.fori_loop(0, columns // tile, body, 0)

    for j in range(n):
        load(j).wait()

    def own_step(m, carry):
        multiply(r_ref.at[m], at, m, True)
        return carry

    lax.fori_loop(0, chunks, own_step, 0)

    def step(i, carry):
        s, m = i // chunks + 1, lax.rem(i, chunks)
        low, high = at - s, at + s

        @pl.when(low >= 0)
        def _():
            push(gathered.at[low, m], low, m, 0, s).wait_recv()

            @pl.when(has_right)
            def _():
                push(gathered.at[low, m], low, m, 0, s).start()

        @pl.when(high < n)
        def _():
            push(gathered.at[high, m], high, m, 1, s).wait_recv()

            @pl.when(has_left)
            def _():
                push(gathered.at[high, m], high, m, 1, s).start()

        @pl.when(low >= 0)
        def _():
            multiply(gathered.at[low, m], low, m, False)

        @pl.when(high < n)
        def _():
            multiply(gathered.at[high, m], high, m, False)

        return carry

    lax.fori_loop(0, (n - 1) * chunks, step, 0)

    def finish(m, carry):
        out_ref[m] = total[m].astype(BF16)
        return carry

    lax.fori_loop(0, chunks, finish, 0)

    def drain(i, carry):
        s, m = i // chunks, lax.rem(i, chunks)

        @pl.when((at - s >= 0) & has_right)
        def _():
            push(r_ref.at[m], at - s, m, 0, s).wait_send()

        @pl.when((at + s < n) & has_left)
        def _():
            push(r_ref.at[m], at + s, m, 1, s).wait_send()

        return carry

    lax.fori_loop(0, n * chunks, drain, 0)


def project(flat, w_out):
    n = lax.axis_size("head")
    chunk = 128
    chunks, depth = flat.shape[0] // chunk, flat.shape[1]
    columns = w_out.shape[1]
    vmem = pl.BlockSpec(memory_space=pltpu.VMEM)
    out = pl.pallas_call(
        functools.partial(project_kernel, n),
        out_shape=jax.ShapeDtypeStruct((chunks, chunk, columns), BF16),
        in_specs=[vmem, pl.BlockSpec(memory_space=pl.ANY)],
        out_specs=vmem,
        scratch_shapes=[
            pltpu.VMEM((n, chunks, chunk, depth), BF16),
            pltpu.VMEM((n, depth, columns), BF16),
            pltpu.VMEM((chunks, chunk, columns), F32),
            pltpu.SemaphoreType.DMA((n,)),
            pltpu.SemaphoreType.DMA((2, n, chunks)),
            pltpu.SemaphoreType.DMA((n, chunks)),
        ],
        compiler_params=pltpu.CompilerParams(
            collective_id=1, has_side_effects=True, vmem_limit_bytes=60 * 2**20
        ),
        name="project",
    )(flat.reshape(chunks, chunk, depth), w_out)
    return out.reshape(chunks * chunk, columns)


def fused(q, k, v, log_decay, prompt_section, q_step, k_step, v_step, step_decay, w_out):
    tokens, heads, hd = q.shape
    rows, steps = q_step.shape[:2]
    sections = lax.axis_size("ctx")
    cumlog = jnp.cumsum(log_decay, axis=1)
    totals = jnp.broadcast_to(cumlog[:, -1][:, None, None], (heads, 8, 128))
    section_ids = prompt_section[:, 0]
    same = section_ids[:, None] == section_ids[None, :]
    ranking = jnp.sum(jnp.where(jnp.tril(same, -1), 1, 0), axis=1)
    slot = (jnp.arange(sections)[:, None, None] * CAP + jnp.arange(CAP)[None, None, :])
    slot = jnp.broadcast_to(slot, (sections, steps, CAP)).reshape(-1)
    slot_step = jnp.broadcast_to(jnp.arange(steps)[None, :, None], (sections, steps, CAP)).reshape(-1)
    row_slot = jnp.tile(section_ids * CAP + ranking, steps)
    row_step = jnp.repeat(jnp.arange(steps), rows)
    pack = (slot[:, None] == row_slot[None, :]) & (slot_step[:, None] == row_step[None, :])
    unpack = (row_slot[:, None] == slot[None, :]) & (row_step[:, None] == slot_step[None, :])
    running = [step_decay[:, 0]]
    for t in range(1, steps):
        running.append(running[-1] + step_decay[:, t])
    step_logs = jnp.stack(running, axis=1)
    step_logs = jnp.transpose(step_logs, (2, 1, 0)).reshape(rows, steps * heads)

    def wide(a):
        return a.reshape(tokens, heads * hd)

    def by_step(a):
        return jnp.transpose(a, (1, 0, 2, 3)).reshape(steps * rows, heads * hd)

    n = lax.axis_size("head")
    chunk = rows * steps
    chunks, depth = tokens // chunk + 1, heads * hd
    vmem = pl.BlockSpec(memory_space=pltpu.VMEM)
    count = sections * CAP * steps
    state = pltpu.VMEM((sections, hd, hd), BF16)
    reads = pltpu.VMEM((sections, count, hd), BF16)
    return pl.pallas_call(
        functools.partial(fused_kernel, sections),
        out_shape=(
            jax.ShapeDtypeStruct((tokens, depth), BF16),
            jax.ShapeDtypeStruct((rows * steps, depth), BF16),
        ),
        in_specs=[vmem] * 12 + [pl.BlockSpec(memory_space=pl.ANY)],
        out_specs=(vmem, vmem),
        scratch_shapes=[
            state, reads, state, reads, pltpu.VMEM((sections, 8, 128), F32),
            state, state, reads, state, reads,
            pltpu.VMEM((n, chunks, chunk, depth), BF16),
            pltpu.VMEM((3, depth, depth), BF16),
            pltpu.VMEM((chunks, chunk, depth), F32),
        ] + [pltpu.SemaphoreType.DMA((sections,))] * 10 + [
            pltpu.SemaphoreType.DMA((4,)),
            pltpu.SemaphoreType.DMA((2, n, chunks)),
            pltpu.SemaphoreType.DMA((n, chunks)),
        ],
        compiler_params=pltpu.CompilerParams(
            collective_id=0, has_side_effects=True, vmem_limit_bytes=62 * 2**20
        ),
        name="fused",
    )(
        wide(q), wide(k), wide(v), cumlog, cumlog.T, totals,
        by_step(q_step), by_step(k_step), by_step(v_step), step_logs,
        pack.astype(BF16), unpack.astype(BF16), w_out,
    )


def entering(value, axis, join, neutral):
    count, mine = (lax.axis_size(axis), lax.axis_index(axis))
    pieces = jax.tree.map(lambda part: lax.all_gather(part, axis), value)
    running = jax.tree.map(
        lambda part, zero: jnp.full_like(part, 0) + jnp.asarray(zero, part.dtype), value, neutral
    )

    def step(position, running):
        longer = join(running, jax.tree.map(lambda part: part[position], pieces))
        return jax.tree.map(lambda new, old: jnp.where(position < mine, new, old), longer, running)

    return lax.fori_loop(0, count - 1, step, running)


def as_sent(value):
    return jax.tree.map(lambda a: a.astype(jnp.bfloat16) if a.dtype == jnp.float32 else a, value)


def split_state(state):
    high_part = state.astype(jnp.bfloat16)
    rest = state - lax.optimization_barrier(high_part).astype(jnp.float32)
    middle_part = rest.astype(jnp.bfloat16)
    low_part = (rest - lax.optimization_barrier(middle_part).astype(jnp.float32)).astype(
        jnp.bfloat16
    )
    return (high_part, middle_part, low_part)


def exact_read(form, query_rows, state):
    parts = split_state(state)
    total = jnp.einsum(form, query_rows, parts[0], preferred_element_type=jnp.float32)
    total = total + jnp.einsum(form, query_rows, parts[1], preferred_element_type=jnp.float32)
    return total + jnp.einsum(form, query_rows, parts[2], preferred_element_type=jnp.float32)


def block_terms(carry_state, query_rows, key_matrix_rows, value_rows, log_rates):
    positions = jnp.arange(log_rates.shape[1])
    causal = positions[:, None] >= positions[None, :]
    cumlog = jnp.cumsum(log_rates, axis=1)
    decays = jnp.where(
        causal[None], jnp.exp(jnp.minimum(cumlog[:, :, None] - cumlog[:, None, :], 0.0)), 0.0
    )
    attention_scores = jnp.einsum(
        "jsv,csv->sjc", query_rows, key_matrix_rows, preferred_element_type=jnp.float32
    )
    weights = (attention_scores * decays).astype(jnp.bfloat16)
    within = jnp.einsum("hnm,mhe->nhe", weights, value_rows, preferred_element_type=jnp.float32)
    carried = exact_read("nhd,hde->nhe", query_rows, carry_state)
    carried = carried * jnp.exp(cumlog).T[:, :, None]
    last_log = cumlog[:, -1]
    weighted_values = (
        key_matrix_rows.astype(jnp.float32) * jnp.exp(last_log[:, None] - cumlog).T[:, :, None]
    ).astype(jnp.bfloat16)
    state_update = jnp.einsum(
        "jxa,jxp->xap", weighted_values, value_rows, preferred_element_type=jnp.float32
    )
    carry_state = jnp.exp(last_log)[:, None, None] * carry_state + state_update
    return (carry_state, within + carried, cumlog)


def combine(earlier, latter):
    return (earlier[0] + latter[0], jnp.exp(latter[0])[:, None, None] * earlier[1] + latter[1])


def retain_gathered(
    q_prompt, k_prompt, v_prompt, log_decay, prompt_section, q_step, k_step, v_step, step_decay
):
    token_count, heads_here, head_dim = q_prompt.shape
    sections = lax.axis_size("ctx")
    carry_state = jnp.zeros((heads_here, head_dim, head_dim), jnp.float32)
    carry_state, partial_value, cumlog = block_terms(
        carry_state, q_prompt, k_prompt, v_prompt, log_decay
    )
    offset = cumlog[:, -1]
    identity = (jnp.zeros_like(offset), jnp.zeros_like(carry_state))
    earlier_log, entry_state = entering((offset, carry_state), "ctx", combine, identity)
    entry_parts = split_state(entry_state)
    entry_read = jnp.einsum(
        "nhd,hde->nhe", q_prompt, entry_parts[0], preferred_element_type=jnp.float32
    )
    entry_read = entry_read + jnp.einsum(
        "nhd,hde->nhe", q_prompt, entry_parts[1], preferred_element_type=jnp.float32
    )
    entry_read = entry_read + jnp.einsum(
        "nhd,hde->nhe", q_prompt, entry_parts[2], preferred_element_type=jnp.float32
    )
    block_out = partial_value + jnp.exp(cumlog).T[:, :, None] * entry_read
    retained = block_out.astype(jnp.bfloat16)
    retention = retained.reshape(token_count, heads_here * head_dim)

    final_state = jnp.exp(offset)[:, None, None] * entry_state + carry_state
    row_count, step_count = (q_step.shape[0], q_step.shape[1])
    section_ids = prompt_section[:, 0]
    owner_hot = (section_ids[:, None] == jnp.arange(sections)[None, :]).astype(jnp.float32)
    before = jnp.tril(jnp.ones((row_count, row_count), jnp.float32), -1)
    counts_before = jnp.dot(before, owner_hot, precision=lax.Precision.HIGHEST)
    ranking = jnp.sum(counts_before * owner_hot, axis=1).astype(jnp.int32)
    slot_ids = section_ids * CAP + ranking
    selector = (jnp.arange(sections * CAP)[:, None] == slot_ids[None, :]).astype(jnp.bfloat16)
    packed = jnp.dot(selector, q_step.reshape(row_count, -1), preferred_element_type=jnp.float32)
    packed = packed.astype(jnp.bfloat16).reshape(sections, CAP, step_count, heads_here, head_dim)
    reads = exact_read(
        "jcthd,jhde->jcthe",
        packed,
        lax.all_gather(as_sent(final_state[None]), "ctx", axis=0, tiled=True),
    )
    slot_reads = reads
    slot_reads = slot_reads.reshape(sections * CAP, step_count, heads_here, head_dim)
    prefix_reads = jnp.take(slot_reads, slot_ids, axis=0)
    step_logs = jnp.cumsum(jnp.transpose(step_decay, (2, 1, 0)), axis=1)
    head_logs = jnp.transpose(step_logs, (0, 2, 1))
    step_index = jnp.arange(step_count)
    causal = step_index[:, None] >= step_index[None, :]
    step_weights = jnp.where(
        causal[None, None],
        jnp.exp(jnp.minimum(head_logs[:, :, :, None] - head_logs[:, :, None, :], 0.0)),
        0.0,
    )
    attention_scores = jnp.einsum(
        "rthd,ruhd->rhtu", q_step, k_step, preferred_element_type=jnp.float32
    )
    own_terms = jnp.einsum(
        "rhtu,ruhe->rthe", attention_scores * step_weights, v_step.astype(jnp.float32)
    )
    step_retention = (jnp.exp(step_logs)[:, :, :, None] * prefix_reads + own_terms).astype(
        jnp.bfloat16
    )
    step_flat = jnp.transpose(step_retention, (1, 0, 2, 3))
    step_flat = step_flat.reshape(row_count * step_count, heads_here * head_dim)
    return jnp.concatenate([retention, step_flat], axis=0)


def shards(
    q_prompt,
    k_prompt,
    v_prompt,
    log_decay,
    prompt_section,
    q_step,
    k_step,
    v_step,
    step_decay,
    w_out,
):
    tokens, heads = q_prompt.shape[:2]
    rows, steps = q_step.shape[:2]
    sections, n = lax.axis_size("ctx"), lax.axis_size("head")
    args = (
        q_prompt, k_prompt, v_prompt, log_decay, prompt_section, q_step, k_step, v_step, step_decay
    )
    if heads == sections and n == 4 and tokens % (rows * steps) == 0:
        prompt_out, step_out = fused(*args, w_out)
    else:
        out = project(retain_gathered(*args), w_out)
        prompt_out, step_out = out[:tokens], out[tokens:]
    step_out = step_out.reshape(steps, rows, w_out.shape[1])
    return (prompt_out, jnp.transpose(step_out, (1, 0, 2)))


def solution(mesh):
    in_specs = (
        P("ctx", "head", None),
        P("ctx", "head", None),
        P("ctx", "head", None),
        P("head", "ctx"),
        P("ctx", None),
        P("ctx", None, "head", None),
        P("ctx", None, "head", None),
        P("ctx", None, "head", None),
        P("head", None, "ctx"),
        P(None, "head"),
    )
    out_specs = (P("ctx", "head"), P("ctx", None, "head"))
    return jax.shard_map(shards, mesh=mesh, in_specs=in_specs, out_specs=out_specs, check_vma=False)
```

```python
import functools
import jax
import jax.numpy as jnp
from jax import lax
from jax.experimental import pallas as pl
from jax.experimental.pallas import tpu as pltpu
from jax.sharding import PartitionSpec as P

CAP = 4
MESH = pl.DeviceIdType.MESH
F32 = jnp.float32
BF16 = jnp.bfloat16


def mm(a, b):
    return jnp.dot(a, b, preferred_element_type=F32)


def fused_kernel(
    sections,
    q_ref, k_ref, v_ref, decay_ref, section_ref,
    qs_ref, ks_ref, vs_ref, step_decay_ref,
    w_ref,
    prompt_ref, step_ref,
    cum_ref, cum_t_ref, total_ref, step_log_ref, pack_ref,
    step_part, state_out, query_out, state_in, query_in, total_in,
    boundary, entry_out, read_out, entry_in, read_in, gathered, weights, total,
    send_s, send_a, send_q, send_e, send_r,
    recv_s, recv_a, recv_q, recv_e, recv_r,
    load_sem, send_z, recv_z,
):
    me = lax.axis_index("ctx")
    at = lax.axis_index("head")
    n = lax.axis_size("head")
    has_left, has_right = at > 0, at < n - 1
    chunks, chunk, depth = total.shape
    parts = chunks - 1
    tile = 512
    far = jnp.where(at < 2, 3, 0)
    near = jnp.where(at == 1, 0, 1)

    def slot_of(j):
        return jnp.where((j == at) | (j == far), 0, jnp.where(j == near, 1, 2))

    def load(j, sem):
        return pltpu.make_async_copy(
            w_ref.at[pl.ds(pl.multiple_of(j * depth, depth), depth)],
            weights.at[slot_of(j)], load_sem.at[sem],
        )

    def pass_on(j, m, way, s):
        return pltpu.make_async_remote_copy(
            src_ref=gathered.at[j, m], dst_ref=gathered.at[j, m],
            send_sem=send_z.at[way, s, m], recv_sem=recv_z.at[j, m],
            device_id={"head": at + 1 if way == 0 else at - 1}, device_id_type=MESH,
        )

    def send_own(m):
        @pl.when(has_right)
        def _():
            pass_on(at, m, 0, 0).start()

        @pl.when(has_left)
        def _():
            pass_on(at, m, 1, 0).start()
    heads = decay_ref.shape[0]
    tokens = q_ref.shape[0]
    hd = q_ref.shape[1] // heads
    rows = section_ref.shape[0]
    steps = qs_ref.shape[0] // rows

    def peer(d):
        return lax.rem(me + d, sections)

    def push(src, dst, send, recv, to):
        return pltpu.make_async_remote_copy(
            src_ref=src, dst_ref=dst, send_sem=send, recv_sem=recv,
            device_id={"ctx": to}, device_id_type=MESH,
        )

    barrier = pltpu.get_barrier_semaphore()
    for d in range(1, sections):
        pl.semaphore_signal(barrier, inc=1, device_id={"ctx": peer(d)}, device_id_type=MESH)

    @pl.when(has_left)
    def _():
        pl.semaphore_signal(barrier, inc=1, device_id={"head": at - 1}, device_id_type=MESH)

    @pl.when(has_right)
    def _():
        pl.semaphore_signal(barrier, inc=1, device_id={"head": at + 1}, device_id_type=MESH)

    other = jnp.where(at == 1, 2, jnp.where(at == 2, 3, 2))
    load(at, 0).start()
    load(near, 1).start()
    load(other, 2).start()

    def lanes(h):
        return slice(h * hd, (h + 1) * hd)

    def iota(shape, axis):
        return lax.broadcasted_iota(jnp.int32, shape, axis)

    def exact(a, b, dims):
        return lax.dot_general(
            a, b, (dims, ((), ())), precision=lax.Precision.HIGHEST, preferred_element_type=F32
        )

    causal = iota((tokens, tokens), 0) >= iota((tokens, tokens), 1)
    ones = causal.astype(F32)
    cum_ref[...] = exact(decay_ref[...], ones, ((1,), (1,)))
    cum_t_ref[...] = exact(ones, decay_ref[...], ((1,), (1,)))
    for h in range(heads):
        total_ref[h] = jnp.broadcast_to(cum_t_ref[tokens - 1:tokens, h:h + 1], (8, 128))

    for h in range(heads):
        column = cum_t_ref[:, h:h + 1]
        keys = (k_ref[:, lanes(h)].astype(F32) * jnp.exp(total_ref[h, 0:1, 0:1] - column)).astype(BF16)
        state_out[h] = lax.dot_general(
            keys, v_ref[:, lanes(h)], (((0,), (0,)), ((), ())), preferred_element_type=F32
        ).astype(BF16)
    pl.semaphore_wait(
        barrier, sections - 1 + has_left.astype(jnp.int32) + has_right.astype(jnp.int32)
    )
    for d in range(1, sections):
        to = peer(d)
        push(total_ref.at[to], total_in.at[me], send_a.at[d], recv_a.at[me], to).start()
        push(state_out.at[to], state_in.at[me], send_s.at[d], recv_s.at[me], to).start()
    state_in[me] = state_out[me]
    total_in[me] = total_ref[me]
    for h in range(heads):
        scores = lax.dot_general(
            q_ref[:, lanes(h)], k_ref[:, lanes(h)], (((1,), (1,)), ((), ())),
            preferred_element_type=F32,
        )
        gap = jnp.minimum(cum_t_ref[:, h:h + 1] - cum_ref[h:h + 1, :], 0.0)
        scaled = jnp.where(causal, scores * jnp.exp(gap), 0.0).astype(BF16)
        total[0:parts, :, lanes(h)] = mm(scaled, v_ref[:, lanes(h)]).reshape(parts, chunk, hd)

    square = (rows, rows)
    section = jnp.broadcast_to(section_ref[...], square)
    across = jnp.sum(jnp.where(iota(square, 0) == iota(square, 1), section, 0), axis=0, keepdims=True)
    earlier = (section == across) & (iota(square, 0) < iota(square, 1))
    ranking = jnp.sum(jnp.where(earlier, 1, 0), axis=0, keepdims=True)
    span = CAP * steps
    base = (iota((sections * CAP, rows), 0) == across * CAP + ranking).astype(BF16)
    wide = (sections * span, sections * CAP)
    spread = (iota(wide, 0) // span == iota(wide, 1) // CAP) & (iota(wide, 0) % CAP == iota(wide, 1) % CAP)
    tall = (rows, rows * steps)
    repeat = (iota(tall, 1) % rows == iota(tall, 0)).astype(BF16)
    full = (sections * span, rows * steps)
    pack = mm(mm(spread.astype(BF16), base).astype(BF16), repeat)
    same_step = iota(full, 0) % span // CAP == iota(full, 1) // rows
    pack_ref[...] = jnp.where(same_step, pack, 0.0).astype(BF16)
    tied = (heads * steps, heads * steps)
    summed = (iota(tied, 0) // steps == iota(tied, 1) % heads) & (iota(tied, 0) % steps <= iota(tied, 1) // heads)
    step_log_ref[...] = exact(step_decay_ref[...], summed.astype(F32), ((0,), (0,)))
    for h in range(heads):
        query_out[h] = mm(pack_ref[...], qs_ref[:, lanes(h)]).astype(BF16)

    for d in range(1, sections):
        frm = peer(d)
        push(total_ref.at[frm], total_in.at[frm], send_a.at[d], recv_a.at[frm], frm).wait_recv()
        push(state_out.at[frm], state_in.at[frm], send_s.at[d], recv_s.at[frm], frm).wait_recv()
    state = jnp.zeros((hd, hd), F32)
    for c in range(sections):
        entry_out[c] = state.astype(BF16)
        state = jnp.exp(total_in[c, 0:1, 0:1]) * state + state_in[c].astype(F32)
        boundary[c] = state.astype(BF16)
    for d in range(1, sections):
        to = peer(d)
        push(entry_out.at[to], entry_in.at[me], send_e.at[d], recv_e.at[me], to).start()
    entry_in[me] = entry_out[me]

    for h in range(heads):
        for t in range(steps):
            here = slice(t * rows, (t + 1) * rows)
            query = qs_ref[here, lanes(h)].astype(F32)
            log_t = step_log_ref[:, t * heads + h:t * heads + h + 1]
            acc = jnp.zeros((rows, hd), F32)
            for u in range(t + 1):
                there = slice(u * rows, (u + 1) * rows)
                score = jnp.sum(query * ks_ref[there, lanes(h)].astype(F32), axis=1, keepdims=True)
                log_u = step_log_ref[:, u * heads + h:u * heads + h + 1]
                weight = score * jnp.exp(jnp.minimum(log_t - log_u, 0.0))
                acc = acc + weight * vs_ref[there, lanes(h)].astype(F32)
            total[parts, here, lanes(h)] = acc

    for d in range(1, sections):
        frm = peer(d)
        push(entry_out.at[frm], entry_in.at[frm], send_e.at[d], recv_e.at[frm], frm).wait_recv()
    for m in range(parts):
        here = slice(m * chunk, (m + 1) * chunk)
        for h in range(heads):
            carried = mm(q_ref[here, lanes(h)], entry_in[h]) * jnp.exp(cum_t_ref[here, h:h + 1])
            gathered[at, m, :, lanes(h)] = (total[m, :, lanes(h)] + carried).astype(BF16)
        send_own(m)

    for d in range(1, sections):
        to = peer(d)
        push(query_out.at[to], query_in.at[me], send_q.at[d], recv_q.at[me], to).start()
    query_in[me] = query_out[me]

    def multiply(j, m, first):
        slot = slot_of(j)

        def body(i, carry):
            cols = pl.ds(pl.multiple_of(i * tile, tile), tile)
            term = mm(gathered[j, m], weights[slot, :, cols])
            if first:
                total[m, :, cols] = term
                return carry

            @pl.when(j != far)
            def _():
                total[m, :, cols] += term

            @pl.when((j == far) & (m < parts))
            def _():
                here = pl.ds(pl.multiple_of(jnp.minimum(m, parts - 1) * chunk, chunk), chunk)
                prompt_ref[here, cols] = (total[m, :, cols] + term).astype(BF16)

            @pl.when((j == far) & (m == parts))
            def _():
                step_ref[:, cols] = (total[m, :, cols] + term).astype(BF16)

            return carry

        lax.fori_loop(0, depth // tile, body, 0)

    def own_step(m, carry):
        multiply(at, m, True)
        return carry

    load(at, 0).wait()
    lax.fori_loop(0, parts // 2, own_step, 0)

    for d in range(1, sections):
        frm = peer(d)
        push(query_out.at[frm], query_in.at[frm], send_q.at[d], recv_q.at[frm], frm).wait_recv()
    for c in range(sections):
        part = slice(c * span, (c + 1) * span)
        asked = query_in[:, part, :].reshape(sections * span, hd)
        read_out[:, part, :] = mm(asked, boundary[c]).astype(BF16).reshape(sections, span, hd)
    for d in range(1, sections):
        to = peer(d)
        push(read_out.at[to], read_in.at[me], send_r.at[d], recv_r.at[me], to).start()
    read_in[me] = read_out[me]

    lax.fori_loop(parts // 2, parts, own_step, 0)

    for d in range(1, sections):
        frm = peer(d)
        push(read_out.at[frm], read_in.at[frm], send_r.at[d], recv_r.at[frm], frm).wait_recv()
    line = (rows * steps, rows * steps)
    order = (iota(line, 1) == iota(line, 0) % steps * rows + iota(line, 0) // steps).astype(BF16)
    for h in range(heads):
        reads = lax.dot_general(
            pack_ref[...], read_in[h], (((0,), (0,)), ((), ())), preferred_element_type=F32
        )
        for t in range(steps):
            here = slice(t * rows, (t + 1) * rows)
            grown = jnp.exp(step_log_ref[:, t * heads + h:t * heads + h + 1])
            step_part[here] = (
                grown * reads[here] + total[parts, here, lanes(h)]
            ).astype(BF16)
        gathered[at, parts, :, lanes(h)] = mm(order, step_part[...]).astype(BF16)
    send_own(parts)

    multiply(at, parts, True)
    load(far, 3).start()
    load(near, 1).wait()
    load(other, 2).wait()
    load(far, 3).wait()

    def step(i, carry):
        s, m = i // chunks + 1, lax.rem(i, chunks)
        low, high = at - s, at + s

        @pl.when(low >= 0)
        def _():
            pass_on(low, m, 0, s).wait_recv()

            @pl.when(has_right)
            def _():
                pass_on(low, m, 0, s).start()

        @pl.when(high < n)
        def _():
            pass_on(high, m, 1, s).wait_recv()

            @pl.when(has_left)
            def _():
                pass_on(high, m, 1, s).start()

        @pl.when(low >= 0)
        def _():
            multiply(low, m, False)

        @pl.when(high < n)
        def _():
            multiply(high, m, False)

        return carry

    lax.fori_loop(0, (n - 1) * chunks, step, 0)

    def drain(i, carry):
        s, m = i // chunks, lax.rem(i, chunks)

        @pl.when((at - s >= 0) & has_right)
        def _():
            pass_on(at - s, m, 0, s).wait_send()

        @pl.when((at + s < n) & has_left)
        def _():
            pass_on(at + s, m, 1, s).wait_send()

        return carry

    lax.fori_loop(0, n * chunks, drain, 0)

    for d in range(1, sections):
        to = peer(d)
        push(total_ref.at[to], total_in.at[me], send_a.at[d], recv_a.at[me], to).wait_send()
        push(state_out.at[to], state_in.at[me], send_s.at[d], recv_s.at[me], to).wait_send()
        push(query_out.at[to], query_in.at[me], send_q.at[d], recv_q.at[me], to).wait_send()
        push(entry_out.at[to], entry_in.at[me], send_e.at[d], recv_e.at[me], to).wait_send()
        push(read_out.at[to], read_in.at[me], send_r.at[d], recv_r.at[me], to).wait_send()


def project_kernel(
    n, r_ref, w_ref, out_ref, gathered, weights, total, load_sem, send_sem, recv_sem
):
    at = lax.axis_index("head")
    chunks, _, depth = r_ref.shape
    columns = w_ref.shape[1]
    tile = min(columns, 512)

    def load(j):
        return pltpu.make_async_copy(
            w_ref.at[pl.ds(pl.multiple_of(j * depth, depth), depth)], weights.at[j], load_sem.at[j]
        )

    def push(src, j, m, way, s):
        return pltpu.make_async_remote_copy(
            src_ref=src, dst_ref=gathered.at[j, m],
            send_sem=send_sem.at[way, s, m], recv_sem=recv_sem.at[j, m],
            device_id={"head": at + 1 if way == 0 else at - 1}, device_id_type=MESH,
        )

    has_left, has_right = at > 0, at < n - 1
    barrier = pltpu.get_barrier_semaphore()

    @pl.when(has_left)
    def _():
        pl.semaphore_signal(barrier, inc=1, device_id={"head": at - 1}, device_id_type=MESH)

    @pl.when(has_right)
    def _():
        pl.semaphore_signal(barrier, inc=1, device_id={"head": at + 1}, device_id_type=MESH)

    pl.semaphore_wait(barrier, has_left.astype(jnp.int32) + has_right.astype(jnp.int32))

    for m in range(chunks):
        @pl.when(has_right)
        def _():
            push(r_ref.at[m], at, m, 0, 0).start()

        @pl.when(has_left)
        def _():
            push(r_ref.at[m], at, m, 1, 0).start()

    for j in range(n):
        load(j).start()

    def multiply(rows, j, m, first):
        def body(i, carry):
            cols = pl.ds(pl.multiple_of(i * tile, tile), tile)
            term = mm(rows[...], weights[j, :, cols])
            if first:
                total[m, :, cols] = term
            else:
                total[m, :, cols] += term
            return carry

        lax.fori_loop(0, columns // tile, body, 0)

    for j in range(n):
        load(j).wait()

    def own_step(m, carry):
        multiply(r_ref.at[m], at, m, True)
        return carry

    lax.fori_loop(0, chunks, own_step, 0)

    def step(i, carry):
        s, m = i // chunks + 1, lax.rem(i, chunks)
        low, high = at - s, at + s

        @pl.when(low >= 0)
        def _():
            push(gathered.at[low, m], low, m, 0, s).wait_recv()

            @pl.when(has_right)
            def _():
                push(gathered.at[low, m], low, m, 0, s).start()

        @pl.when(high < n)
        def _():
            push(gathered.at[high, m], high, m, 1, s).wait_recv()

            @pl.when(has_left)
            def _():
                push(gathered.at[high, m], high, m, 1, s).start()

        @pl.when(low >= 0)
        def _():
            multiply(gathered.at[low, m], low, m, False)

        @pl.when(high < n)
        def _():
            multiply(gathered.at[high, m], high, m, False)

        return carry

    lax.fori_loop(0, (n - 1) * chunks, step, 0)

    def finish(m, carry):
        out_ref[m] = total[m].astype(BF16)
        return carry

    lax.fori_loop(0, chunks, finish, 0)

    def drain(i, carry):
        s, m = i // chunks, lax.rem(i, chunks)

        @pl.when((at - s >= 0) & has_right)
        def _():
            push(r_ref.at[m], at - s, m, 0, s).wait_send()

        @pl.when((at + s < n) & has_left)
        def _():
            push(r_ref.at[m], at + s, m, 1, s).wait_send()

        return carry

    lax.fori_loop(0, n * chunks, drain, 0)


def project(flat, w_out):
    n = lax.axis_size("head")
    chunk = 128
    chunks, depth = flat.shape[0] // chunk, flat.shape[1]
    columns = w_out.shape[1]
    vmem = pl.BlockSpec(memory_space=pltpu.VMEM)
    out = pl.pallas_call(
        functools.partial(project_kernel, n),
        out_shape=jax.ShapeDtypeStruct((chunks, chunk, columns), BF16),
        in_specs=[vmem, pl.BlockSpec(memory_space=pl.ANY)],
        out_specs=vmem,
        scratch_shapes=[
            pltpu.VMEM((n, chunks, chunk, depth), BF16),
            pltpu.VMEM((n, depth, columns), BF16),
            pltpu.VMEM((chunks, chunk, columns), F32),
            pltpu.SemaphoreType.DMA((n,)),
            pltpu.SemaphoreType.DMA((2, n, chunks)),
            pltpu.SemaphoreType.DMA((n, chunks)),
        ],
        compiler_params=pltpu.CompilerParams(
            collective_id=1, has_side_effects=True, vmem_limit_bytes=60 * 2**20
        ),
        name="project",
    )(flat.reshape(chunks, chunk, depth), w_out)
    return out.reshape(chunks * chunk, columns)


def fused(q, k, v, log_decay, prompt_section, q_step, k_step, v_step, step_decay, w_out):
    tokens, heads, hd = q.shape
    rows, steps = q_step.shape[:2]
    sections = lax.axis_size("ctx")
    def wide(a):
        return a.reshape(tokens, heads * hd)

    def by_step(a):
        return jnp.transpose(a, (1, 0, 2, 3)).reshape(steps * rows, heads * hd)

    n = lax.axis_size("head")
    chunk = rows * steps
    chunks, depth = tokens // chunk + 1, heads * hd
    vmem = pl.BlockSpec(memory_space=pltpu.VMEM)
    count = sections * CAP * steps
    state = pltpu.VMEM((sections, hd, hd), BF16)
    reads = pltpu.VMEM((sections, count, hd), BF16)
    return pl.pallas_call(
        functools.partial(fused_kernel, sections),
        out_shape=(
            jax.ShapeDtypeStruct((tokens, depth), BF16),
            jax.ShapeDtypeStruct((rows * steps, depth), BF16),
        ),
        in_specs=[vmem] * 9 + [pl.BlockSpec(memory_space=pl.ANY)],
        out_specs=(vmem, vmem),
        scratch_shapes=[
            pltpu.VMEM((heads, tokens), F32),
            pltpu.VMEM((tokens, heads), F32),
            pltpu.VMEM((heads, 8, 128), F32),
            pltpu.VMEM((rows, heads * steps), F32),
            pltpu.VMEM((count, rows * steps), BF16),
            pltpu.VMEM((rows * steps, hd), BF16),
            state, reads, state, reads, pltpu.VMEM((sections, 8, 128), F32),
            state, state, reads, state, reads,
            pltpu.VMEM((n, chunks, chunk, depth), BF16),
            pltpu.VMEM((3, depth, depth), BF16),
            pltpu.VMEM((chunks, chunk, depth), F32),
        ] + [pltpu.SemaphoreType.DMA((sections,))] * 10 + [
            pltpu.SemaphoreType.DMA((4,)),
            pltpu.SemaphoreType.DMA((2, n, chunks)),
            pltpu.SemaphoreType.DMA((n, chunks)),
        ],
        compiler_params=pltpu.CompilerParams(
            collective_id=0, has_side_effects=True, vmem_limit_bytes=62 * 2**20
        ),
        name="fused",
    )(
        wide(q), wide(k), wide(v), log_decay, prompt_section,
        by_step(q_step), by_step(k_step), by_step(v_step),
        step_decay.reshape(heads * steps, rows), w_out,
    )


def entering(value, axis, join, neutral):
    count, mine = (lax.axis_size(axis), lax.axis_index(axis))
    pieces = jax.tree.map(lambda part: lax.all_gather(part, axis), value)
    running = jax.tree.map(
        lambda part, zero: jnp.full_like(part, 0) + jnp.asarray(zero, part.dtype), value, neutral
    )

    def step(position, running):
        longer = join(running, jax.tree.map(lambda part: part[position], pieces))
        return jax.tree.map(lambda new, old: jnp.where(position < mine, new, old), longer, running)

    return lax.fori_loop(0, count - 1, step, running)


def as_sent(value):
    return jax.tree.map(lambda a: a.astype(jnp.bfloat16) if a.dtype == jnp.float32 else a, value)


def split_state(state):
    high_part = state.astype(jnp.bfloat16)
    rest = state - lax.optimization_barrier(high_part).astype(jnp.float32)
    middle_part = rest.astype(jnp.bfloat16)
    low_part = (rest - lax.optimization_barrier(middle_part).astype(jnp.float32)).astype(
        jnp.bfloat16
    )
    return (high_part, middle_part, low_part)


def exact_read(form, query_rows, state):
    parts = split_state(state)
    total = jnp.einsum(form, query_rows, parts[0], preferred_element_type=jnp.float32)
    total = total + jnp.einsum(form, query_rows, parts[1], preferred_element_type=jnp.float32)
    return total + jnp.einsum(form, query_rows, parts[2], preferred_element_type=jnp.float32)


def block_terms(carry_state, query_rows, key_matrix_rows, value_rows, log_rates):
    positions = jnp.arange(log_rates.shape[1])
    causal = positions[:, None] >= positions[None, :]
    cumlog = jnp.cumsum(log_rates, axis=1)
    decays = jnp.where(
        causal[None], jnp.exp(jnp.minimum(cumlog[:, :, None] - cumlog[:, None, :], 0.0)), 0.0
    )
    attention_scores = jnp.einsum(
        "jsv,csv->sjc", query_rows, key_matrix_rows, preferred_element_type=jnp.float32
    )
    weights = (attention_scores * decays).astype(jnp.bfloat16)
    within = jnp.einsum("hnm,mhe->nhe", weights, value_rows, preferred_element_type=jnp.float32)
    carried = exact_read("nhd,hde->nhe", query_rows, carry_state)
    carried = carried * jnp.exp(cumlog).T[:, :, None]
    last_log = cumlog[:, -1]
    weighted_values = (
        key_matrix_rows.astype(jnp.float32) * jnp.exp(last_log[:, None] - cumlog).T[:, :, None]
    ).astype(jnp.bfloat16)
    state_update = jnp.einsum(
        "jxa,jxp->xap", weighted_values, value_rows, preferred_element_type=jnp.float32
    )
    carry_state = jnp.exp(last_log)[:, None, None] * carry_state + state_update
    return (carry_state, within + carried, cumlog)


def combine(earlier, latter):
    return (earlier[0] + latter[0], jnp.exp(latter[0])[:, None, None] * earlier[1] + latter[1])


def retain_gathered(
    q_prompt, k_prompt, v_prompt, log_decay, prompt_section, q_step, k_step, v_step, step_decay
):
    token_count, heads_here, head_dim = q_prompt.shape
    sections = lax.axis_size("ctx")
    carry_state = jnp.zeros((heads_here, head_dim, head_dim), jnp.float32)
    carry_state, partial_value, cumlog = block_terms(
        carry_state, q_prompt, k_prompt, v_prompt, log_decay
    )
    offset = cumlog[:, -1]
    identity = (jnp.zeros_like(offset), jnp.zeros_like(carry_state))
    earlier_log, entry_state = entering((offset, carry_state), "ctx", combine, identity)
    entry_parts = split_state(entry_state)
    entry_read = jnp.einsum(
        "nhd,hde->nhe", q_prompt, entry_parts[0], preferred_element_type=jnp.float32
    )
    entry_read = entry_read + jnp.einsum(
        "nhd,hde->nhe", q_prompt, entry_parts[1], preferred_element_type=jnp.float32
    )
    entry_read = entry_read + jnp.einsum(
        "nhd,hde->nhe", q_prompt, entry_parts[2], preferred_element_type=jnp.float32
    )
    block_out = partial_value + jnp.exp(cumlog).T[:, :, None] * entry_read
    retained = block_out.astype(jnp.bfloat16)
    retention = retained.reshape(token_count, heads_here * head_dim)

    final_state = jnp.exp(offset)[:, None, None] * entry_state + carry_state
    row_count, step_count = (q_step.shape[0], q_step.shape[1])
    section_ids = prompt_section[:, 0]
    owner_hot = (section_ids[:, None] == jnp.arange(sections)[None, :]).astype(jnp.float32)
    before = jnp.tril(jnp.ones((row_count, row_count), jnp.float32), -1)
    counts_before = jnp.dot(before, owner_hot, precision=lax.Precision.HIGHEST)
    ranking = jnp.sum(counts_before * owner_hot, axis=1).astype(jnp.int32)
    slot_ids = section_ids * CAP + ranking
    selector = (jnp.arange(sections * CAP)[:, None] == slot_ids[None, :]).astype(jnp.bfloat16)
    packed = jnp.dot(selector, q_step.reshape(row_count, -1), preferred_element_type=jnp.float32)
    packed = packed.astype(jnp.bfloat16).reshape(sections, CAP, step_count, heads_here, head_dim)
    reads = exact_read(
        "jcthd,jhde->jcthe",
        packed,
        lax.all_gather(as_sent(final_state[None]), "ctx", axis=0, tiled=True),
    )
    slot_reads = reads
    slot_reads = slot_reads.reshape(sections * CAP, step_count, heads_here, head_dim)
    prefix_reads = jnp.take(slot_reads, slot_ids, axis=0)
    step_logs = jnp.cumsum(jnp.transpose(step_decay, (2, 1, 0)), axis=1)
    head_logs = jnp.transpose(step_logs, (0, 2, 1))
    step_index = jnp.arange(step_count)
    causal = step_index[:, None] >= step_index[None, :]
    step_weights = jnp.where(
        causal[None, None],
        jnp.exp(jnp.minimum(head_logs[:, :, :, None] - head_logs[:, :, None, :], 0.0)),
        0.0,
    )
    attention_scores = jnp.einsum(
        "rthd,ruhd->rhtu", q_step, k_step, preferred_element_type=jnp.float32
    )
    own_terms = jnp.einsum(
        "rhtu,ruhe->rthe", attention_scores * step_weights, v_step.astype(jnp.float32)
    )
    step_retention = (jnp.exp(step_logs)[:, :, :, None] * prefix_reads + own_terms).astype(
        jnp.bfloat16
    )
    step_flat = jnp.transpose(step_retention, (1, 0, 2, 3))
    step_flat = step_flat.reshape(row_count * step_count, heads_here * head_dim)
    return jnp.concatenate([retention, step_flat], axis=0)


def shards(
    q_prompt,
    k_prompt,
    v_prompt,
    log_decay,
    prompt_section,
    q_step,
    k_step,
    v_step,
    step_decay,
    w_out,
):
    tokens, heads = q_prompt.shape[:2]
    rows, steps = q_step.shape[:2]
    sections, n = lax.axis_size("ctx"), lax.axis_size("head")
    args = (
        q_prompt, k_prompt, v_prompt, log_decay, prompt_section, q_step, k_step, v_step, step_decay
    )
    if heads == sections and n == 4 and tokens % (rows * steps) == 0:
        prompt_out, step_out = fused(*args, w_out)
        return (prompt_out, step_out.reshape(rows, steps, w_out.shape[1]))
    out = project(retain_gathered(*args), w_out)
    step_out = out[tokens:].reshape(steps, rows, w_out.shape[1])
    return (out[:tokens], jnp.transpose(step_out, (1, 0, 2)))


def solution(mesh):
    in_specs = (
        P("ctx", "head", None),
        P("ctx", "head", None),
        P("ctx", "head", None),
        P("head", "ctx"),
        P("ctx", None),
        P("ctx", None, "head", None),
        P("ctx", None, "head", None),
        P("ctx", None, "head", None),
        P("head", None, "ctx"),
        P(None, "head"),
    )
    out_specs = (P("ctx", "head"), P("ctx", None, "head"))
    return jax.shard_map(shards, mesh=mesh, in_specs=in_specs, out_specs=out_specs, check_vma=False)
```

```python
import functools
import jax
import jax.numpy as jnp
from jax import lax
from jax.experimental import pallas as pl
from jax.experimental.pallas import tpu as pltpu
from jax.sharding import PartitionSpec as P

CAP = 4
MESH = pl.DeviceIdType.MESH
F32 = jnp.float32
BF16 = jnp.bfloat16


def mm(a, b):
    return jnp.dot(a, b, preferred_element_type=F32)


def fused_kernel(
    sections,
    q_ref, k_ref, v_ref, decay_ref, section_ref,
    qs_ref, ks_ref, vs_ref, step_decay_ref,
    w_ref,
    prompt_ref, step_ref,
    cum_ref, cum_t_ref, total_ref, step_log_ref, pack_ref,
    step_part, state_out, query_out, state_in, query_in, total_in,
    boundary, entry_out, read_out, entry_in, read_in, gathered, weights, total,
    send_s, send_a, send_q, send_e, send_r,
    recv_s, recv_a, recv_q, recv_e, recv_r,
    load_sem, send_z, recv_z,
):
    me = lax.axis_index("ctx")
    at = lax.axis_index("head")
    n = lax.axis_size("head")
    has_left, has_right = at > 0, at < n - 1
    chunks, chunk, depth = total.shape
    parts = chunks - 1
    tile = 512
    far = jnp.where(at < 2, 3, 0)
    near = jnp.where(at == 1, 0, 1)

    def slot_of(j):
        return jnp.where((j == at) | (j == far), 0, jnp.where(j == near, 1, 2))

    def load(j, sem):
        return pltpu.make_async_copy(
            w_ref.at[pl.ds(pl.multiple_of(j * depth, depth), depth)],
            weights.at[slot_of(j)], load_sem.at[sem],
        )

    def pass_on(j, m, way, s):
        return pltpu.make_async_remote_copy(
            src_ref=gathered.at[j, m], dst_ref=gathered.at[j, m],
            send_sem=send_z.at[way, s, m], recv_sem=recv_z.at[j, m],
            device_id={"head": at + 1 if way == 0 else at - 1}, device_id_type=MESH,
        )

    def send_own(m):
        @pl.when(has_right)
        def _():
            pass_on(at, m, 0, 0).start()

        @pl.when(has_left)
        def _():
            pass_on(at, m, 1, 0).start()
    heads = decay_ref.shape[0]
    tokens = q_ref.shape[0]
    hd = q_ref.shape[1] // heads
    rows = section_ref.shape[0]
    steps = qs_ref.shape[0] // rows

    def peer(d):
        return lax.rem(me + d, sections)

    def push(src, dst, send, recv, to):
        return pltpu.make_async_remote_copy(
            src_ref=src, dst_ref=dst, send_sem=send, recv_sem=recv,
            device_id={"ctx": to}, device_id_type=MESH,
        )

    barrier = pltpu.get_barrier_semaphore()
    for d in range(1, sections):
        pl.semaphore_signal(barrier, inc=1, device_id={"ctx": peer(d)}, device_id_type=MESH)

    @pl.when(has_left)
    def _():
        pl.semaphore_signal(barrier, inc=1, device_id={"head": at - 1}, device_id_type=MESH)

    @pl.when(has_right)
    def _():
        pl.semaphore_signal(barrier, inc=1, device_id={"head": at + 1}, device_id_type=MESH)

    other = jnp.where(at == 1, 2, jnp.where(at == 2, 3, 2))
    load(at, 0).start()
    load(near, 1).start()
    load(other, 2).start()

    def lanes(h):
        return slice(h * hd, (h + 1) * hd)

    def iota(shape, axis):
        return lax.broadcasted_iota(jnp.int32, shape, axis)

    def exact(a, b, dims):
        return lax.dot_general(
            a, b, (dims, ((), ())), precision=lax.Precision.HIGHEST, preferred_element_type=F32
        )

    causal = iota((tokens, tokens), 0) >= iota((tokens, tokens), 1)
    ones = causal.astype(F32)
    cum_t_ref[...] = exact(ones, decay_ref[...], ((1,), (1,)))
    for h in range(heads):
        total_ref[h] = jnp.broadcast_to(cum_t_ref[tokens - 1:tokens, h:h + 1], (8, 128))

    for h in range(heads):
        column = cum_t_ref[:, h:h + 1]
        keys = (k_ref[:, lanes(h)].astype(F32) * jnp.exp(total_ref[h, 0:1, 0:1] - column)).astype(BF16)
        state_out[h] = lax.dot_general(
            keys, v_ref[:, lanes(h)], (((0,), (0,)), ((), ())), preferred_element_type=F32
        ).astype(BF16)
    pl.semaphore_wait(
        barrier, sections - 1 + has_left.astype(jnp.int32) + has_right.astype(jnp.int32)
    )
    for d in range(1, sections):
        to = peer(d)
        push(total_ref.at[to], total_in.at[me], send_a.at[d], recv_a.at[me], to).start()
        push(state_out.at[to], state_in.at[me], send_s.at[d], recv_s.at[me], to).start()
    state_in[me] = state_out[me]
    total_in[me] = total_ref[me]
    cum_ref[...] = exact(decay_ref[...], ones, ((1,), (1,)))
    for h in range(heads):
        scores = lax.dot_general(
            q_ref[:, lanes(h)], k_ref[:, lanes(h)], (((1,), (1,)), ((), ())),
            preferred_element_type=F32,
        )
        gap = jnp.minimum(cum_t_ref[:, h:h + 1] - cum_ref[h:h + 1, :], 0.0)
        scaled = jnp.where(causal, scores * jnp.exp(gap), 0.0).astype(BF16)
        total[0:parts, :, lanes(h)] = mm(scaled, v_ref[:, lanes(h)]).reshape(parts, chunk, hd)

    square = (rows, rows)
    section = jnp.broadcast_to(section_ref[...], square)
    across = jnp.sum(jnp.where(iota(square, 0) == iota(square, 1), section, 0), axis=0, keepdims=True)
    earlier = (section == across) & (iota(square, 0) < iota(square, 1))
    ranking = jnp.sum(jnp.where(earlier, 1, 0), axis=0, keepdims=True)
    span = CAP * steps
    base = (iota((sections * CAP, rows), 0) == across * CAP + ranking).astype(BF16)
    wide = (sections * span, sections * CAP)
    spread = (iota(wide, 0) // span == iota(wide, 1) // CAP) & (iota(wide, 0) % CAP == iota(wide, 1) % CAP)
    tall = (rows, rows * steps)
    repeat = (iota(tall, 1) % rows == iota(tall, 0)).astype(BF16)
    full = (sections * span, rows * steps)
    pack = mm(mm(spread.astype(BF16), base).astype(BF16), repeat)
    same_step = iota(full, 0) % span // CAP == iota(full, 1) // rows
    pack_ref[...] = jnp.where(same_step, pack, 0.0).astype(BF16)
    tied = (heads * steps, heads * steps)
    summed = (iota(tied, 0) // steps == iota(tied, 1) % heads) & (iota(tied, 0) % steps <= iota(tied, 1) // heads)
    step_log_ref[...] = exact(step_decay_ref[...], summed.astype(F32), ((0,), (0,)))
    for h in range(heads):
        query_out[h] = mm(pack_ref[...], qs_ref[:, lanes(h)]).astype(BF16)

    for d in range(1, sections):
        frm = peer(d)
        push(total_ref.at[frm], total_in.at[frm], send_a.at[d], recv_a.at[frm], frm).wait_recv()
        push(state_out.at[frm], state_in.at[frm], send_s.at[d], recv_s.at[frm], frm).wait_recv()
    state = jnp.zeros((hd, hd), F32)
    for c in range(sections):
        entry_out[c] = state.astype(BF16)
        state = jnp.exp(total_in[c, 0:1, 0:1]) * state + state_in[c].astype(F32)
        boundary[c] = state.astype(BF16)

        @pl.when(me != c)
        def _():
            gap = lax.rem(c - me + sections, sections)
            push(entry_out.at[c], entry_in.at[me], send_e.at[gap], recv_e.at[me], c).start()

    entry_in[me] = entry_out[me]

    for h in range(heads):
        for t in range(steps):
            here = slice(t * rows, (t + 1) * rows)
            query = qs_ref[here, lanes(h)].astype(F32)
            log_t = step_log_ref[:, t * heads + h:t * heads + h + 1]
            acc = jnp.zeros((rows, hd), F32)
            for u in range(t + 1):
                there = slice(u * rows, (u + 1) * rows)
                score = jnp.sum(query * ks_ref[there, lanes(h)].astype(F32), axis=1, keepdims=True)
                log_u = step_log_ref[:, u * heads + h:u * heads + h + 1]
                weight = score * jnp.exp(jnp.minimum(log_t - log_u, 0.0))
                acc = acc + weight * vs_ref[there, lanes(h)].astype(F32)
            total[parts, here, lanes(h)] = acc

    for d in range(1, sections):
        frm = peer(d)
        push(entry_out.at[frm], entry_in.at[frm], send_e.at[d], recv_e.at[frm], frm).wait_recv()
    for m in range(parts):
        here = slice(m * chunk, (m + 1) * chunk)
        for h in range(heads):
            carried = mm(q_ref[here, lanes(h)], entry_in[h]) * jnp.exp(cum_t_ref[here, h:h + 1])
            gathered[at, m, :, lanes(h)] = (total[m, :, lanes(h)] + carried).astype(BF16)
        send_own(m)

    for d in range(1, sections):
        to = peer(d)
        push(query_out.at[to], query_in.at[me], send_q.at[d], recv_q.at[me], to).start()
    query_in[me] = query_out[me]

    def multiply(j, m, first):
        slot = slot_of(j)

        def body(i, carry):
            cols = pl.ds(pl.multiple_of(i * tile, tile), tile)
            term = mm(gathered[j, m], weights[slot, :, cols])
            if first:
                total[m, :, cols] = term
                return carry

            @pl.when(j != far)
            def _():
                total[m, :, cols] += term

            @pl.when((j == far) & (m < parts))
            def _():
                here = pl.ds(pl.multiple_of(jnp.minimum(m, parts - 1) * chunk, chunk), chunk)
                prompt_ref[here, cols] = (total[m, :, cols] + term).astype(BF16)

            @pl.when((j == far) & (m == parts))
            def _():
                step_ref[:, cols] = (total[m, :, cols] + term).astype(BF16)

            return carry

        lax.fori_loop(0, depth // tile, body, 0)

    def own_step(m, carry):
        multiply(at, m, True)
        return carry

    load(at, 0).wait()
    lax.fori_loop(0, parts // 2, own_step, 0)

    for d in range(1, sections):
        frm = peer(d)
        push(query_out.at[frm], query_in.at[frm], send_q.at[d], recv_q.at[frm], frm).wait_recv()
    for c in range(sections):
        part = slice(c * span, (c + 1) * span)
        asked = query_in[:, part, :].reshape(sections * span, hd)
        read_out[:, part, :] = mm(asked, boundary[c]).astype(BF16).reshape(sections, span, hd)
    for d in range(1, sections):
        to = peer(d)
        push(read_out.at[to], read_in.at[me], send_r.at[d], recv_r.at[me], to).start()
    read_in[me] = read_out[me]

    lax.fori_loop(parts // 2, parts, own_step, 0)

    for d in range(1, sections):
        frm = peer(d)
        push(read_out.at[frm], read_in.at[frm], send_r.at[d], recv_r.at[frm], frm).wait_recv()
    line = (rows * steps, rows * steps)
    order = (iota(line, 1) == iota(line, 0) % steps * rows + iota(line, 0) // steps).astype(BF16)
    for h in range(heads):
        reads = lax.dot_general(
            pack_ref[...], read_in[h], (((0,), (0,)), ((), ())), preferred_element_type=F32
        )
        for t in range(steps):
            here = slice(t * rows, (t + 1) * rows)
            grown = jnp.exp(step_log_ref[:, t * heads + h:t * heads + h + 1])
            step_part[here] = (
                grown * reads[here] + total[parts, here, lanes(h)]
            ).astype(BF16)
        gathered[at, parts, :, lanes(h)] = mm(order, step_part[...]).astype(BF16)
    send_own(parts)

    multiply(at, parts, True)
    load(far, 3).start()
    load(near, 1).wait()
    load(other, 2).wait()
    load(far, 3).wait()

    def step(i, carry):
        s, m = i // chunks + 1, lax.rem(i, chunks)
        low, high = at - s, at + s

        @pl.when(low >= 0)
        def _():
            pass_on(low, m, 0, s).wait_recv()

            @pl.when(has_right)
            def _():
                pass_on(low, m, 0, s).start()

        @pl.when(high < n)
        def _():
            pass_on(high, m, 1, s).wait_recv()

            @pl.when(has_left)
            def _():
                pass_on(high, m, 1, s).start()

        @pl.when(low >= 0)
        def _():
            multiply(low, m, False)

        @pl.when(high < n)
        def _():
            multiply(high, m, False)

        return carry

    lax.fori_loop(0, (n - 1) * chunks, step, 0)

    def drain(i, carry):
        s, m = i // chunks, lax.rem(i, chunks)

        @pl.when((at - s >= 0) & has_right)
        def _():
            pass_on(at - s, m, 0, s).wait_send()

        @pl.when((at + s < n) & has_left)
        def _():
            pass_on(at + s, m, 1, s).wait_send()

        return carry

    lax.fori_loop(0, n * chunks, drain, 0)

    for d in range(1, sections):
        to = peer(d)
        push(total_ref.at[to], total_in.at[me], send_a.at[d], recv_a.at[me], to).wait_send()
        push(state_out.at[to], state_in.at[me], send_s.at[d], recv_s.at[me], to).wait_send()
        push(query_out.at[to], query_in.at[me], send_q.at[d], recv_q.at[me], to).wait_send()
        push(entry_out.at[to], entry_in.at[me], send_e.at[d], recv_e.at[me], to).wait_send()
        push(read_out.at[to], read_in.at[me], send_r.at[d], recv_r.at[me], to).wait_send()


def project_kernel(
    n, r_ref, w_ref, out_ref, gathered, weights, total, load_sem, send_sem, recv_sem
):
    at = lax.axis_index("head")
    chunks, _, depth = r_ref.shape
    columns = w_ref.shape[1]
    tile = min(columns, 512)

    def load(j):
        return pltpu.make_async_copy(
            w_ref.at[pl.ds(pl.multiple_of(j * depth, depth), depth)], weights.at[j], load_sem.at[j]
        )

    def push(src, j, m, way, s):
        return pltpu.make_async_remote_copy(
            src_ref=src, dst_ref=gathered.at[j, m],
            send_sem=send_sem.at[way, s, m], recv_sem=recv_sem.at[j, m],
            device_id={"head": at + 1 if way == 0 else at - 1}, device_id_type=MESH,
        )

    has_left, has_right = at > 0, at < n - 1
    barrier = pltpu.get_barrier_semaphore()

    @pl.when(has_left)
    def _():
        pl.semaphore_signal(barrier, inc=1, device_id={"head": at - 1}, device_id_type=MESH)

    @pl.when(has_right)
    def _():
        pl.semaphore_signal(barrier, inc=1, device_id={"head": at + 1}, device_id_type=MESH)

    pl.semaphore_wait(barrier, has_left.astype(jnp.int32) + has_right.astype(jnp.int32))

    for m in range(chunks):
        @pl.when(has_right)
        def _():
            push(r_ref.at[m], at, m, 0, 0).start()

        @pl.when(has_left)
        def _():
            push(r_ref.at[m], at, m, 1, 0).start()

    for j in range(n):
        load(j).start()

    def multiply(rows, j, m, first):
        def body(i, carry):
            cols = pl.ds(pl.multiple_of(i * tile, tile), tile)
            term = mm(rows[...], weights[j, :, cols])
            if first:
                total[m, :, cols] = term
            else:
                total[m, :, cols] += term
            return carry

        lax.fori_loop(0, columns // tile, body, 0)

    for j in range(n):
        load(j).wait()

    def own_step(m, carry):
        multiply(r_ref.at[m], at, m, True)
        return carry

    lax.fori_loop(0, chunks, own_step, 0)

    def step(i, carry):
        s, m = i // chunks + 1, lax.rem(i, chunks)
        low, high = at - s, at + s

        @pl.when(low >= 0)
        def _():
            push(gathered.at[low, m], low, m, 0, s).wait_recv()

            @pl.when(has_right)
            def _():
                push(gathered.at[low, m], low, m, 0, s).start()

        @pl.when(high < n)
        def _():
            push(gathered.at[high, m], high, m, 1, s).wait_recv()

            @pl.when(has_left)
            def _():
                push(gathered.at[high, m], high, m, 1, s).start()

        @pl.when(low >= 0)
        def _():
            multiply(gathered.at[low, m], low, m, False)

        @pl.when(high < n)
        def _():
            multiply(gathered.at[high, m], high, m, False)

        return carry

    lax.fori_loop(0, (n - 1) * chunks, step, 0)

    def finish(m, carry):
        out_ref[m] = total[m].astype(BF16)
        return carry

    lax.fori_loop(0, chunks, finish, 0)

    def drain(i, carry):
        s, m = i // chunks, lax.rem(i, chunks)

        @pl.when((at - s >= 0) & has_right)
        def _():
            push(r_ref.at[m], at - s, m, 0, s).wait_send()

        @pl.when((at + s < n) & has_left)
        def _():
            push(r_ref.at[m], at + s, m, 1, s).wait_send()

        return carry

    lax.fori_loop(0, n * chunks, drain, 0)


def project(flat, w_out):
    n = lax.axis_size("head")
    chunk = 128
    chunks, depth = flat.shape[0] // chunk, flat.shape[1]
    columns = w_out.shape[1]
    vmem = pl.BlockSpec(memory_space=pltpu.VMEM)
    out = pl.pallas_call(
        functools.partial(project_kernel, n),
        out_shape=jax.ShapeDtypeStruct((chunks, chunk, columns), BF16),
        in_specs=[vmem, pl.BlockSpec(memory_space=pl.ANY)],
        out_specs=vmem,
        scratch_shapes=[
            pltpu.VMEM((n, chunks, chunk, depth), BF16),
            pltpu.VMEM((n, depth, columns), BF16),
            pltpu.VMEM((chunks, chunk, columns), F32),
            pltpu.SemaphoreType.DMA((n,)),
            pltpu.SemaphoreType.DMA((2, n, chunks)),
            pltpu.SemaphoreType.DMA((n, chunks)),
        ],
        compiler_params=pltpu.CompilerParams(
            collective_id=1, has_side_effects=True, vmem_limit_bytes=60 * 2**20
        ),
        name="project",
    )(flat.reshape(chunks, chunk, depth), w_out)
    return out.reshape(chunks * chunk, columns)


def fused(q, k, v, log_decay, prompt_section, q_step, k_step, v_step, step_decay, w_out):
    tokens, heads, hd = q.shape
    rows, steps = q_step.shape[:2]
    sections = lax.axis_size("ctx")
    def wide(a):
        return a.reshape(tokens, heads * hd)

    def by_step(a):
        return jnp.transpose(a, (1, 0, 2, 3)).reshape(steps * rows, heads * hd)

    n = lax.axis_size("head")
    chunk = rows * steps
    chunks, depth = tokens // chunk + 1, heads * hd
    vmem = pl.BlockSpec(memory_space=pltpu.VMEM)
    count = sections * CAP * steps
    state = pltpu.VMEM((sections, hd, hd), BF16)
    reads = pltpu.VMEM((sections, count, hd), BF16)
    return pl.pallas_call(
        functools.partial(fused_kernel, sections),
        out_shape=(
            jax.ShapeDtypeStruct((tokens, depth), BF16),
            jax.ShapeDtypeStruct((rows * steps, depth), BF16),
        ),
        in_specs=[vmem] * 9 + [pl.BlockSpec(memory_space=pl.ANY)],
        out_specs=(vmem, vmem),
        scratch_shapes=[
            pltpu.VMEM((heads, tokens), F32),
            pltpu.VMEM((tokens, heads), F32),
            pltpu.VMEM((heads, 8, 128), F32),
            pltpu.VMEM((rows, heads * steps), F32),
            pltpu.VMEM((count, rows * steps), BF16),
            pltpu.VMEM((rows * steps, hd), BF16),
            state, reads, state, reads, pltpu.VMEM((sections, 8, 128), F32),
            state, state, reads, state, reads,
            pltpu.VMEM((n, chunks, chunk, depth), BF16),
            pltpu.VMEM((3, depth, depth), BF16),
            pltpu.VMEM((chunks, chunk, depth), F32),
        ] + [pltpu.SemaphoreType.DMA((sections,))] * 10 + [
            pltpu.SemaphoreType.DMA((4,)),
            pltpu.SemaphoreType.DMA((2, n, chunks)),
            pltpu.SemaphoreType.DMA((n, chunks)),
        ],
        compiler_params=pltpu.CompilerParams(
            collective_id=0, has_side_effects=True, vmem_limit_bytes=62 * 2**20
        ),
        name="fused",
    )(
        wide(q), wide(k), wide(v), log_decay, prompt_section,
        by_step(q_step), by_step(k_step), by_step(v_step),
        step_decay.reshape(heads * steps, rows), w_out,
    )


def entering(value, axis, join, neutral):
    count, mine = (lax.axis_size(axis), lax.axis_index(axis))
    pieces = jax.tree.map(lambda part: lax.all_gather(part, axis), value)
    running = jax.tree.map(
        lambda part, zero: jnp.full_like(part, 0) + jnp.asarray(zero, part.dtype), value, neutral
    )

    def step(position, running):
        longer = join(running, jax.tree.map(lambda part: part[position], pieces))
        return jax.tree.map(lambda new, old: jnp.where(position < mine, new, old), longer, running)

    return lax.fori_loop(0, count - 1, step, running)


def as_sent(value):
    return jax.tree.map(lambda a: a.astype(jnp.bfloat16) if a.dtype == jnp.float32 else a, value)


def split_state(state):
    high_part = state.astype(jnp.bfloat16)
    rest = state - lax.optimization_barrier(high_part).astype(jnp.float32)
    middle_part = rest.astype(jnp.bfloat16)
    low_part = (rest - lax.optimization_barrier(middle_part).astype(jnp.float32)).astype(
        jnp.bfloat16
    )
    return (high_part, middle_part, low_part)


def exact_read(form, query_rows, state):
    parts = split_state(state)
    total = jnp.einsum(form, query_rows, parts[0], preferred_element_type=jnp.float32)
    total = total + jnp.einsum(form, query_rows, parts[1], preferred_element_type=jnp.float32)
    return total + jnp.einsum(form, query_rows, parts[2], preferred_element_type=jnp.float32)


def block_terms(carry_state, query_rows, key_matrix_rows, value_rows, log_rates):
    positions = jnp.arange(log_rates.shape[1])
    causal = positions[:, None] >= positions[None, :]
    cumlog = jnp.cumsum(log_rates, axis=1)
    decays = jnp.where(
        causal[None], jnp.exp(jnp.minimum(cumlog[:, :, None] - cumlog[:, None, :], 0.0)), 0.0
    )
    attention_scores = jnp.einsum(
        "jsv,csv->sjc", query_rows, key_matrix_rows, preferred_element_type=jnp.float32
    )
    weights = (attention_scores * decays).astype(jnp.bfloat16)
    within = jnp.einsum("hnm,mhe->nhe", weights, value_rows, preferred_element_type=jnp.float32)
    carried = exact_read("nhd,hde->nhe", query_rows, carry_state)
    carried = carried * jnp.exp(cumlog).T[:, :, None]
    last_log = cumlog[:, -1]
    weighted_values = (
        key_matrix_rows.astype(jnp.float32) * jnp.exp(last_log[:, None] - cumlog).T[:, :, None]
    ).astype(jnp.bfloat16)
    state_update = jnp.einsum(
        "jxa,jxp->xap", weighted_values, value_rows, preferred_element_type=jnp.float32
    )
    carry_state = jnp.exp(last_log)[:, None, None] * carry_state + state_update
    return (carry_state, within + carried, cumlog)


def combine(earlier, latter):
    return (earlier[0] + latter[0], jnp.exp(latter[0])[:, None, None] * earlier[1] + latter[1])


def retain_gathered(
    q_prompt, k_prompt, v_prompt, log_decay, prompt_section, q_step, k_step, v_step, step_decay
):
    token_count, heads_here, head_dim = q_prompt.shape
    sections = lax.axis_size("ctx")
    carry_state = jnp.zeros((heads_here, head_dim, head_dim), jnp.float32)
    carry_state, partial_value, cumlog = block_terms(
        carry_state, q_prompt, k_prompt, v_prompt, log_decay
    )
    offset = cumlog[:, -1]
    identity = (jnp.zeros_like(offset), jnp.zeros_like(carry_state))
    earlier_log, entry_state = entering((offset, carry_state), "ctx", combine, identity)
    entry_parts = split_state(entry_state)
    entry_read = jnp.einsum(
        "nhd,hde->nhe", q_prompt, entry_parts[0], preferred_element_type=jnp.float32
    )
    entry_read = entry_read + jnp.einsum(
        "nhd,hde->nhe", q_prompt, entry_parts[1], preferred_element_type=jnp.float32
    )
    entry_read = entry_read + jnp.einsum(
        "nhd,hde->nhe", q_prompt, entry_parts[2], preferred_element_type=jnp.float32
    )
    block_out = partial_value + jnp.exp(cumlog).T[:, :, None] * entry_read
    retained = block_out.astype(jnp.bfloat16)
    retention = retained.reshape(token_count, heads_here * head_dim)

    final_state = jnp.exp(offset)[:, None, None] * entry_state + carry_state
    row_count, step_count = (q_step.shape[0], q_step.shape[1])
    section_ids = prompt_section[:, 0]
    owner_hot = (section_ids[:, None] == jnp.arange(sections)[None, :]).astype(jnp.float32)
    before = jnp.tril(jnp.ones((row_count, row_count), jnp.float32), -1)
    counts_before = jnp.dot(before, owner_hot, precision=lax.Precision.HIGHEST)
    ranking = jnp.sum(counts_before * owner_hot, axis=1).astype(jnp.int32)
    slot_ids = section_ids * CAP + ranking
    selector = (jnp.arange(sections * CAP)[:, None] == slot_ids[None, :]).astype(jnp.bfloat16)
    packed = jnp.dot(selector, q_step.reshape(row_count, -1), preferred_element_type=jnp.float32)
    packed = packed.astype(jnp.bfloat16).reshape(sections, CAP, step_count, heads_here, head_dim)
    reads = exact_read(
        "jcthd,jhde->jcthe",
        packed,
        lax.all_gather(as_sent(final_state[None]), "ctx", axis=0, tiled=True),
    )
    slot_reads = reads
    slot_reads = slot_reads.reshape(sections * CAP, step_count, heads_here, head_dim)
    prefix_reads = jnp.take(slot_reads, slot_ids, axis=0)
    step_logs = jnp.cumsum(jnp.transpose(step_decay, (2, 1, 0)), axis=1)
    head_logs = jnp.transpose(step_logs, (0, 2, 1))
    step_index = jnp.arange(step_count)
    causal = step_index[:, None] >= step_index[None, :]
    step_weights = jnp.where(
        causal[None, None],
        jnp.exp(jnp.minimum(head_logs[:, :, :, None] - head_logs[:, :, None, :], 0.0)),
        0.0,
    )
    attention_scores = jnp.einsum(
        "rthd,ruhd->rhtu", q_step, k_step, preferred_element_type=jnp.float32
    )
    own_terms = jnp.einsum(
        "rhtu,ruhe->rthe", attention_scores * step_weights, v_step.astype(jnp.float32)
    )
    step_retention = (jnp.exp(step_logs)[:, :, :, None] * prefix_reads + own_terms).astype(
        jnp.bfloat16
    )
    step_flat = jnp.transpose(step_retention, (1, 0, 2, 3))
    step_flat = step_flat.reshape(row_count * step_count, heads_here * head_dim)
    return jnp.concatenate([retention, step_flat], axis=0)


def shards(
    q_prompt,
    k_prompt,
    v_prompt,
    log_decay,
    prompt_section,
    q_step,
    k_step,
    v_step,
    step_decay,
    w_out,
):
    tokens, heads = q_prompt.shape[:2]
    rows, steps = q_step.shape[:2]
    sections, n = lax.axis_size("ctx"), lax.axis_size("head")
    args = (
        q_prompt, k_prompt, v_prompt, log_decay, prompt_section, q_step, k_step, v_step, step_decay
    )
    if heads == sections and n == 4 and tokens % (rows * steps) == 0:
        prompt_out, step_out = fused(*args, w_out)
        return (prompt_out, step_out.reshape(rows, steps, w_out.shape[1]))
    out = project(retain_gathered(*args), w_out)
    step_out = out[tokens:].reshape(steps, rows, w_out.shape[1])
    return (out[:tokens], jnp.transpose(step_out, (1, 0, 2)))


def solution(mesh):
    in_specs = (
        P("ctx", "head", None),
        P("ctx", "head", None),
        P("ctx", "head", None),
        P("head", "ctx"),
        P("ctx", None),
        P("ctx", None, "head", None),
        P("ctx", None, "head", None),
        P("ctx", None, "head", None),
        P("head", None, "ctx"),
        P(None, "head"),
    )
    out_specs = (P("ctx", "head"), P("ctx", None, "head"))
    return jax.shard_map(shards, mesh=mesh, in_specs=in_specs, out_specs=out_specs, check_vma=False)
```
